256 devices in a mesh: blk: 64 (over y, z_hi, x), head: 4 (over z_lo, core).
Axes of the slice: x: 4, y: 4, z: 8 (z_hi: 4, z_lo: 2; z = z_hi * 2 + z_lo), core: 2. Of those that a mesh axis runs over, the one named last changes fastest.
Arguments:
- queries: bfloat16 [49152, 5120], P(('blk', 'head')), may hold values from -6 to 6
- key_input: bfloat16 [49152, 5120], P(('blk', 'head')), may hold values from -6 to 6
- value_input: bfloat16 [49152, 5120], P(('blk', 'head')), may hold values from -6 to 6
- token_order: int32 [49152], P('blk'), may hold values from 0 to 49151, as said below
- tile_mask: int32 [128, 128], P('blk'), may hold values from 0 to 1, as said below
Outputs:
- attended: bfloat16 [49152, 5120], P(('blk', 'head'))
The draws below stay inside these ranges and needn't reach their ends.
Inputs may be any that keep to these rules, and one draw needn't show every extreme that they name: Within each aligned block of 768 positions, token_order is a permutation of the raster positions of that same block. tile_mask[i, j] is 1 whenever i // 2 = j // 2, and also whenever i // 2 is odd and j = i - 1 or j = i + 1; it is 0 whenever i // 2 and j // 2 differ by more than 1.
All inputs are finite; a program needn't handle non-finite values.
Results may differ from the reference program's by a relative error of at most 0.0047.
Values may be sent and summed in bfloat16 or wider, within the bound.
A program may use at most 128 MiB of HBM per device.

```python
import math
import jax
import jax.numpy as jnp
from jax import lax

HEADS = 40
HEAD_DIM = 128
D = 5120
TILE = 384
TILES_DEV = 2
TILES = 128
TOKENS = 49152


def draw_queries(key, part):
    key = jax.random.fold_in(key, 11)
    base = jnp.clip(jax.random.normal(key, (TOKENS, HEADS * HEAD_DIM), jnp.float32), -6.0, 6.0)
    return base.astype(jnp.bfloat16)


def draw_key_input(key, part):
    key = jax.random.fold_in(key, 12)
    base = jnp.clip(jax.random.normal(key, (TOKENS, HEADS * HEAD_DIM), jnp.float32), -6.0, 6.0)
    return base.astype(jnp.bfloat16)


def draw_token_order(key, part):
    key = jax.random.fold_in(key, 21)
    group_rows = TILES_DEV * TILE
    count = TOKENS // group_rows

    def one_block(index):
        return jax.random.permutation(jax.random.fold_in(key, index), group_rows).astype(jnp.int32)
    blocks = jax.vmap(one_block)(jnp.arange(count, dtype=jnp.int32))
    offsets = (jnp.arange(count, dtype=jnp.int32) * group_rows)[:, None]
    return (blocks + offsets).reshape(TOKENS)


def draw_tile_mask(key, part):
    key = jax.random.fold_in(key, 31)
    first, second = jax.random.split(key)
    row_tile = jnp.arange(TILES)[:, None]
    col_tile = jnp.arange(TILES)[None, :]
    row_run = row_tile // TILES_DEV
    col_run = col_tile // TILES_DEV
    same = row_run == col_run
    near = jnp.abs(row_run - col_run) == 1
    adjacent = (row_run % 2 == 1) & (jnp.abs(row_tile - col_tile) == 1)
    threshold = jax.random.randint(first, (TILES, 1), 0, 100)
    rolled = jax.random.randint(second, (TILES, TILES), 0, 100)
    chosen = jnp.where(same | adjacent, 1, jnp.where(near & (rolled < threshold), 1, 0))
    return chosen.astype(jnp.int32)


def levels(key, extent, cuts, smallest, largest):
    def one(position, parts):
        heights = jax.random.uniform(jax.random.fold_in(jax.random.fold_in(key, 6), position), (parts,), jnp.float32, smallest / len(cuts), largest / len(cuts))
        return jnp.repeat(jnp.exp(heights), extent[position] // parts).reshape((-1,) + (1,) * (len(extent) - position - 1))

    gain = one(*cuts[0])
    for cut in cuts[1:]:
        gain = gain * one(*cut)
    return gain


def scatter_about(stream_key, dims, scale, bound, pieces=(), held_as=jnp.bfloat16):
    gain = levels(stream_key, dims, pieces, -0.22, 0.18) if pieces else 1.0
    drawn = jax.random.normal(stream_key, dims, jnp.float32) * scale * gain
    return jnp.minimum(jnp.maximum(drawn, -bound), bound).astype(held_as)


def setup_inputs(seed: int = 0) -> dict:
    arg_keys = jax.random.split(jax.random.key(seed), 6)
    queries = draw_queries(jax.random.fold_in(arg_keys[5], 71), 0)
    key_input = draw_key_input(jax.random.fold_in(arg_keys[5], 71), 0)
    value_input = scatter_about(arg_keys[2], (TOKENS, D), 1.0, 6.0, ((0, 256),))
    token_order = draw_token_order(jax.random.fold_in(arg_keys[5], 71), 0)
    tile_mask = draw_tile_mask(jax.random.fold_in(arg_keys[5], 71), 0)
    return dict(queries=queries, key_input=key_input, value_input=value_input, token_order=token_order, tile_mask=tile_mask)


def reference(queries, key_input, value_input, token_order, tile_mask):
    group_rows = TILES_DEV * TILE
    width = HEADS * HEAD_DIM
    scale = 1.0 / math.sqrt(HEAD_DIM)
    query_sorted = jnp.take(queries, token_order, axis=0)
    key_sorted = jnp.take(key_input, token_order, axis=0)
    value_sorted = jnp.take(value_input, token_order, axis=0)
    padding = jnp.zeros((group_rows, width), jnp.bfloat16)
    key_padded = jnp.concatenate((padding, key_sorted, padding), axis=0)
    value_padded = jnp.concatenate((padding, value_sorted, padding), axis=0)
    mask_padded = jnp.pad(tile_mask, ((0, 0), (TILES_DEV, TILES_DEV)))

    def one_group(index):
        start = index * group_rows
        query_block = lax.dynamic_slice_in_dim(query_sorted, start, group_rows, 0)
        query_block = query_block.reshape(group_rows, HEADS, HEAD_DIM).astype(jnp.float32)
        key_block = lax.dynamic_slice_in_dim(key_padded, start, 3 * group_rows, 0)
        key_block = key_block.reshape(3 * group_rows, HEADS, HEAD_DIM).astype(jnp.float32)
        value_block = lax.dynamic_slice_in_dim(value_padded, start, 3 * group_rows, 0)
        value_block = value_block.reshape(3 * group_rows, HEADS, HEAD_DIM).astype(jnp.float32)
        tile_rows = lax.dynamic_slice(mask_padded, (index * TILES_DEV, index * TILES_DEV), (TILES_DEV, 3 * TILES_DEV))
        visible = jnp.repeat(jnp.repeat(tile_rows > 0, TILE, axis=0), TILE, axis=1)
        scores = jnp.einsum('qhd,khd->hqk', query_block, key_block) * scale
        scores = jnp.where(visible[None], scores, -jnp.inf)
        top = lax.optimization_barrier(jnp.max(scores, axis=2, keepdims=True))
        weights = jnp.exp(scores - top)
        total = lax.optimization_barrier(jnp.sum(weights, axis=2))
        rounded = lax.optimization_barrier(weights.astype(jnp.bfloat16)).astype(jnp.float32)
        mixed = jnp.einsum('hqk,khd->qhd', rounded, value_block)
        result = mixed / jnp.transpose(total)[:, :, None]
        return result.astype(jnp.bfloat16).reshape(group_rows, width)
    blocks = lax.map(one_group, jnp.arange(TILES // TILES_DEV, dtype=jnp.int32))
    ordered = blocks.reshape(TOKENS, width)
    return jnp.zeros_like(queries).at[token_order].set(ordered)
```

```python
import functools
import math

import jax
import jax.numpy as jnp
from jax import lax
from jax.experimental import pallas as pl
from jax.experimental.pallas import tpu as pltpu
from jax.sharding import PartitionSpec as P

HEAD_DIM = 128
ROW = 4
PEERS = 2 * ROW
LANES = 128
HIDE = -(2.0**100)
MESH = pl.DeviceIdType.MESH


def kernel(
    heads, runs,
    q_in, k_in, v_in, order_ref, mask_ref,
    out,
    kbuf, vbuf, qbuf, obuf, info, km, qm, top_s, sum_s, acc_s,
    x_recv, x_send, z_recv, z_send, h_recv, h_send, o_recv, o_send, i_recv, i_send, ih_recv, ih_send,
):
    rows = q_in.shape[0]
    run_len = 4 * rows
    half = 2 * rows
    factor = math.log2(math.e) / math.sqrt(HEAD_DIM)

    blk = lax.axis_index("blk")
    head = lax.axis_index("head")
    x = lax.rem(blk, ROW)
    first = blk - x
    zl = lax.div(head, 2)
    core = lax.rem(head, 2)
    me = 2 * x + core
    quarter = head
    after = lax.rem(blk + ROW, runs)
    before = lax.rem(blk + runs - ROW, runs)
    halo_blk = lax.rem(blk + runs + (2 * zl - 1) * ROW, runs)
    halo_src = 1 + 3 * zl
    halo_dst = 5 - 5 * zl
    halo_side = 1 - zl

    def device(peer):
        return (first + lax.div(peer, 2), 2 * zl + lax.rem(peer, 2))

    partner = (blk, 2 * (1 - zl) + core)

    def peer_at(step):
        return lax.rem(me + step, PEERS)

    barrier = pltpu.get_barrier_semaphore()
    for step in range(1, PEERS):
        pl.semaphore_signal(barrier, inc=1, device_id=device(peer_at(step)), device_id_type=MESH)
    pl.semaphore_signal(barrier, inc=1, device_id=partner, device_id_type=MESH)
    pl.semaphore_signal(barrier, inc=1, device_id=(after, core), device_id_type=MESH)
    pl.semaphore_signal(barrier, inc=1, device_id=(before, 2 + core), device_id_type=MESH)
    pl.semaphore_wait(barrier, PEERS + 2)

    def columns(peer, j):
        return pl.ds(pl.multiple_of((heads * peer + j) * HEAD_DIM, HEAD_DIM), HEAD_DIM)

    def send(src, dst, send_sem, recv_sem, to):
        pltpu.make_async_remote_copy(
            src_ref=src, dst_ref=dst, send_sem=send_sem, recv_sem=recv_sem, device_id=to, device_id_type=MESH
        ).start()

    def wait(like, sem):
        pltpu.make_async_copy(like, like, sem).wait()

    def slab(buf, j):
        return buf.at[j, pl.ds(1, ROW), pl.ds(2 * zl, 2)]

    def partner_slab(buf, j):
        return buf.at[j, pl.ds(1, ROW), pl.ds(2 * (1 - zl), 2)]

    def x_start(j):
        for kind, (source, buf) in enumerate(((k_in, kbuf), (v_in, vbuf), (q_in, qbuf))):
            place = qbuf.at[j, me] if kind == 2 else buf.at[j, 1 + x, quarter]
            pltpu.make_async_copy(source.at[:, columns(me, j)], place, x_recv.at[kind, j]).start()
            for step in range(1, PEERS):
                peer = peer_at(step)
                send(
                    source.at[:, columns(peer, j)], place,
                    x_send.at[kind, j], x_recv.at[kind, j], device(peer),
                )

    x_start(0)

    order = (order_ref[...] - blk * run_len).astype(jnp.float32)
    order = jnp.transpose(jnp.broadcast_to(order, (LANES, run_len)))[half:]
    lane = lax.broadcasted_iota(jnp.int32, (half, LANES), 1).astype(jnp.float32)
    second = jnp.concatenate(
        [
            jnp.sum(jnp.where(order == lane + LANES * g, 1.0, 0.0), axis=0, keepdims=True)
            for g in range(run_len // LANES)
        ],
        axis=1,
    )
    seen = mask_ref[...].astype(jnp.float32)
    mask_lane = lax.broadcasted_iota(jnp.int32, seen.shape, 1)

    def bias(offset):
        column = jnp.sum(jnp.where(mask_lane == 2 * blk + offset, seen, 0.0), axis=1, keepdims=True)
        return HIDE * (1.0 - (column[0:1] + second * (column[1:2] - column[0:1])))

    which = lax.broadcasted_iota(jnp.int32, (16, run_len), 0)

    def stack(parts):
        total = jnp.zeros((16, run_len), jnp.float32)
        for index, part in enumerate(parts):
            total = jnp.where(which == index, part, total)
        return total.astype(jnp.bfloat16)

    mine = info.at[1 + x]
    mine[0:16] = stack((1.0 - second, second, 1.0 - second, second))
    mine[16:32] = stack((bias(-2), bias(-1), bias(2), bias(3)))
    for step in range(1, ROW):
        to = (first + lax.rem(x + step, ROW), head)
        send(mine, mine, i_send, i_recv, to)

    def spread(values):
        tall = jnp.concatenate([values, jnp.zeros((LANES - 16, run_len), jnp.float32)], axis=0)
        return jnp.transpose(tall).astype(jnp.bfloat16)

    def key_marks(slot):
        km[slot] = spread(info[slot, 0:16].astype(jnp.float32))

    def halo_start(kind, buf, j):
        for target in range(2):
            send(
                buf.at[j, halo_src], buf.at[j, halo_dst],
                h_send.at[kind, j], h_recv.at[halo_side, kind, j], (halo_blk, 2 * target + core),
            )

    def query(j, r):
        return qbuf[j, pl.ds(2 * r, 2)].reshape(half, HEAD_DIM)

    def add_run(state, j, r, slot, side):
        top, total, acc = state
        q = query(j, r)
        k = kbuf[j, slot].reshape(run_len, HEAD_DIM)
        v = vbuf[j, slot].reshape(run_len, HEAD_DIM)
        if side is not None:
            marks = qm[side, r, pl.ds(pl.multiple_of(zl * half, half), half)]
            q = jnp.concatenate([q, marks], axis=1)
            k = jnp.concatenate([k, km[slot]], axis=1)
        scores = lax.dot_general(q, k, (((1,), (1,)), ((), ())), preferred_element_type=jnp.float32) * factor
        high = jnp.max(scores, axis=1, keepdims=True)
        new = high if top is None else jnp.maximum(top, high)
        weights = jnp.exp2(scores - new)
        part = jnp.sum(weights, axis=1, keepdims=True)
        mixed = jnp.dot(weights.astype(jnp.bfloat16), v, preferred_element_type=jnp.float32)
        if top is None:
            return new, part, mixed
        fade = jnp.exp2(top - new)
        return new, total * fade + part, acc * fade + mixed

    def finish(state, j, r):
        _, total, acc = state
        obuf[j, pl.ds(2 * r, 2)] = (acc / total).astype(jnp.bfloat16).reshape(2, rows, HEAD_DIM)

    def send_out(j, peers):
        for peer in peers:
            @pl.when(peer != me)
            def _():
                send(obuf.at[j, peer], out.at[:, columns(me, j)], o_send.at[j], o_recv, device(peer))

            @pl.when(peer == me)
            def _():
                pltpu.make_async_copy(obuf.at[j, peer], out.at[:, columns(me, j)], o_recv).start()

    def keep(state, edge):
        top, total, acc = state
        top_s[edge] = jnp.broadcast_to(top, (half, LANES))
        sum_s[edge] = jnp.broadcast_to(total, (half, LANES))
        acc_s[edge] = acc

    def kept(edge):
        return top_s[edge][:, 0:1], sum_s[edge][:, 0:1], acc_s[edge]

    nothing = (None, None, None)

    def inner(j):
        keep(add_run(add_run(nothing, j, 0, 1, None), j, 0, 2, 1), 0)
        keep(add_run(add_run(nothing, j, 3, 4, None), j, 3, 3, 0), 1)

        def middle(r, carry):
            state = add_run(nothing, j, r, r + 1, None)
            state = add_run(state, j, r, r, 0)
            state = add_run(state, j, r, r + 2, 1)
            finish(state, j, r)
            return carry

        lax.fori_loop(1, 3, middle, 0)
        send_out(j, [2 + lax.rem(me + step, 4) for step in range(4)])

    def edges(j):
        finish(add_run(kept(0), j, 0, 0, 0), j, 0)
        finish(add_run(kept(1), j, 3, 5, 1), j, 3)
        send_out(j, [lax.rem(6 + lax.rem(me + step, 4), PEERS) for step in range(4)])

    def one_head(j, carry):
        @pl.when(j < heads)
        def _():
            for kind, buf in enumerate((kbuf, vbuf)):
                wait(slab(buf, j), x_recv.at[kind, j])
                send(slab(buf, j), slab(buf, j), z_send.at[kind, j], z_recv.at[kind, j], partner)

        @pl.when(j + 1 < heads)
        def _():
            x_start(j + 1)

        @pl.when(j == 0)
        def _():
            wait(info.at[pl.ds(0, ROW - 1)], i_recv)
            for target in range(2):
                send(
                    info.at[halo_src], info.at[halo_dst],
                    ih_send, ih_recv.at[halo_side], (halo_blk, 2 * target + core),
                )
            for r in range(ROW):
                key_marks(1 + r)
                marks = info[1 + r, 16:32].astype(jnp.float32)
                qm[0, r] = spread(jnp.where(which < 2, marks, 0.0))
                qm[1, r] = spread(jnp.where(which >= 2, marks, 0.0))

        @pl.when(j > 0)
        def _():
            @pl.when(j == 1)
            def _():
                wait(info.at[0], ih_recv.at[0])
                wait(info.at[5], ih_recv.at[1])
                key_marks(0)
                key_marks(5)

            for side, slot in ((0, 0), (1, 5)):
                for kind, buf in enumerate((kbuf, vbuf)):
                    wait(buf.at[j - 1, slot], h_recv.at[side, kind, j - 1])
            edges(j - 1)

        @pl.when(j < heads)
        def _():
            for kind, buf in enumerate((kbuf, vbuf)):
                wait(partner_slab(buf, j), z_recv.at[kind, j])
                halo_start(kind, buf, j)
            wait(qbuf.at[j], x_recv.at[2, j])
            inner(j)

        return carry

    lax.fori_loop(0, heads + 1, one_head, 0)

    wait(out, o_recv)
    wait(info.at[pl.ds(0, ROW - 1)], i_send)
    wait(info.at[pl.ds(0, 2)], ih_send)

    def drain(j, carry):
        for kind, buf in enumerate((kbuf, vbuf, qbuf)):
            wait(qbuf.at[j, pl.ds(0, PEERS - 1)], x_send.at[kind, j])
            if kind < 2:
                wait(slab(buf, j), z_send.at[kind, j])
                wait(buf.at[j, pl.ds(0, 2)], h_send.at[kind, j])
        wait(qbuf.at[j, pl.ds(0, PEERS - 1)], o_send.at[j])
        return carry

    lax.fori_loop(0, heads, drain, 0)


def local(queries, key_input, value_input, token_order, tile_mask):
    rows, width = queries.shape
    heads = width // HEAD_DIM // PEERS
    runs = lax.axis_size("blk")
    run_len = 4 * rows
    half = 2 * rows
    bf16, f32 = jnp.bfloat16, jnp.float32
    dma = pltpu.SemaphoreType.DMA
    hbm = pl.BlockSpec(memory_space=pl.ANY)
    vmem = pl.BlockSpec(memory_space=pltpu.VMEM)
    flops = 4 * heads * ROW * half * 3 * run_len * HEAD_DIM
    return pl.pallas_call(
        functools.partial(kernel, heads, runs),
        out_shape=jax.ShapeDtypeStruct(queries.shape, queries.dtype),
        in_specs=[hbm, hbm, hbm, vmem, vmem],
        out_specs=hbm,
        scratch_shapes=[
            pltpu.VMEM((heads, 6, 4, rows, HEAD_DIM), bf16),
            pltpu.VMEM((heads, 6, 4, rows, HEAD_DIM), bf16),
            pltpu.VMEM((heads, PEERS, rows, HEAD_DIM), bf16),
            pltpu.VMEM((heads, PEERS, rows, HEAD_DIM), bf16),
            pltpu.VMEM((6, 32, run_len), bf16),
            pltpu.VMEM((6, run_len, LANES), bf16),
            pltpu.VMEM((2, ROW, run_len, LANES), bf16),
            pltpu.VMEM((2, half, LANES), f32),
            pltpu.VMEM((2, half, LANES), f32),
            pltpu.VMEM((2, half, HEAD_DIM), f32),
            dma((3, heads)), dma((3, heads)),
            dma((2, heads)), dma((2, heads)),
            dma((2, 2, heads)), dma((2, heads)),
            dma, dma((heads,)),
            dma, dma,
            dma((2,)), dma,
        ],
        compiler_params=pltpu.CompilerParams(
            collective_id=0, has_side_effects=True, vmem_limit_bytes=56 * 1024 * 1024
        ),
        cost_estimate=pl.CostEstimate(
            flops=flops, bytes_accessed=8 * rows * width, transcendentals=flops // (4 * HEAD_DIM)
        ),
    )(queries, key_input, value_input, token_order.reshape(1, run_len), tile_mask)


def solution(mesh):
    in_specs = (
        P(("blk", "head"), None),
        P(("blk", "head"), None),
        P(("blk", "head"), None),
        P("blk"),
        P("blk", None),
    )
    out_specs = P(("blk", "head"), None)
    return jax.shard_map(local, mesh=mesh, in_specs=in_specs, out_specs=out_specs, check_vma=False)
```

```python
import functools
import math

import jax
import jax.numpy as jnp
from jax import lax
from jax.experimental import pallas as pl
from jax.experimental.pallas import tpu as pltpu
from jax.sharding import PartitionSpec as P

HEAD_DIM = 128
ROW = 4
PEERS = 2 * ROW
LANES = 128
HIDE = -(2.0**100)
MESH = pl.DeviceIdType.MESH


def kernel(
    heads, runs,
    q_in, k_in, v_in, order_ref, mask_ref,
    out,
    kbuf, vbuf, qbuf, obuf, q_far, o_far, o_back, log_far, log_back, info, km, qm, top_s, sum_s, acc_s,
    x_recv, x_send, z_recv, z_send, d_send, h_recv, h_send, o_recv, o_send, i_recv, i_send, ih_recv, ih_send,
    q_recv, q_send, p_recv, p_send, l_recv, l_send,
):
    rows = q_in.shape[0]
    run_len = 4 * rows
    half = 2 * rows
    factor = math.log2(math.e) / math.sqrt(HEAD_DIM)
    last = ROW - 1

    blk = lax.axis_index("blk")
    head = lax.axis_index("head")
    x = lax.rem(blk, ROW)
    first = blk - x
    zl = lax.div(head, 2)
    core = lax.rem(head, 2)
    me = 2 * x + core
    across = 2 * (1 - zl)
    partner = (blk, across + core)
    mate = (lax.rem(blk + runs + (2 * zl - 1) * ROW, runs), across + core)
    own_edge = last * zl
    far_edge = last * (1 - zl)

    def device(peer):
        return (first + lax.div(peer, 2), 2 * zl + lax.rem(peer, 2))

    def peer_at(step):
        return lax.rem(me + step, PEERS)

    barrier = pltpu.get_barrier_semaphore()
    greet = [device(peer_at(step)) for step in range(1, PEERS)]
    greet += [partner, (blk, across + 1 - core), mate]
    for to in greet:
        pl.semaphore_signal(barrier, inc=1, device_id=to, device_id_type=MESH)
    pl.semaphore_wait(barrier, len(greet))

    def columns(peer, j):
        return pl.ds(pl.multiple_of((heads * peer + j) * HEAD_DIM, HEAD_DIM), HEAD_DIM)

    def send(src, dst, send_sem, recv_sem, to):
        pltpu.make_async_remote_copy(
            src_ref=src, dst_ref=dst, send_sem=send_sem, recv_sem=recv_sem, device_id=to, device_id_type=MESH
        ).start()

    def wait(like, sem):
        pltpu.make_async_copy(like, like, sem).wait()

    sources = ((0, k_in, kbuf), (1, v_in, vbuf), (2, q_in, qbuf))

    def direct_start(j):
        for kind, source, buf in sources[:2]:
            for c in range(2):
                send(
                    source.at[:, columns(2 * x + c, j)], buf.at[j, x, head],
                    d_send.at[kind, j], z_recv.at[kind, j, x], (blk, across + c),
                )

    def x_start(j):
        for kind, source, buf in sources:
            place = qbuf.at[j, me] if kind == 2 else buf.at[j, x, head]
            pltpu.make_async_copy(source.at[:, columns(me, j)], place, x_recv.at[kind, j, x]).start()
            for step in range(1, PEERS):
                peer = peer_at(step)
                send(
                    source.at[:, columns(peer, j)], place,
                    x_send.at[kind, j], x_recv.at[kind, j, x], device(peer),
                )

    def unit(buf, j, run, side):
        return buf.at[j, run, pl.ds(2 * side, 2)]

    def z_start(j, run):
        for kind, _, buf in sources[:2]:
            wait(unit(buf, j, run, zl), x_recv.at[kind, j, run])

            @pl.when(run != x)
            def _():
                send(
                    unit(buf, j, run, zl), unit(buf, j, run, zl),
                    z_send.at[kind, j, run], z_recv.at[kind, j, run], partner,
                )

    def queries_of(j, run):
        return qbuf.at[j, pl.ds(2 * run, 2)]

    def q_start(j):
        for run in range(ROW):
            wait(queries_of(j, run), x_recv.at[2, j, run])
        send(queries_of(j, far_edge), q_far.at[j], q_send.at[j], q_recv.at[j], partner)

    direct_start(0)
    x_start(0)
    for j in range(1, heads):
        direct_start(j)

    order = (order_ref[...] - blk * run_len).astype(jnp.float32)
    order = jnp.transpose(jnp.broadcast_to(order, (LANES, run_len)))[half:]
    lane = lax.broadcasted_iota(jnp.int32, (half, LANES), 1).astype(jnp.float32)
    second = jnp.concatenate(
        [
            jnp.sum(jnp.where(order == lane + LANES * g, 1.0, 0.0), axis=0, keepdims=True)
            for g in range(run_len // LANES)
        ],
        axis=1,
    )
    seen = mask_ref[...].astype(jnp.float32)
    mask_lane = lax.broadcasted_iota(jnp.int32, seen.shape, 1)

    def bias(offset):
        column = jnp.sum(jnp.where(mask_lane == 2 * blk + offset, seen, 0.0), axis=1, keepdims=True)
        return HIDE * (1.0 - (column[0:1] + second * (column[1:2] - column[0:1])))

    which = lax.broadcasted_iota(jnp.int32, (16, run_len), 0)

    def stack(parts):
        total = jnp.zeros((16, run_len), jnp.float32)
        for index, part in enumerate(parts):
            total = jnp.where(which == index, part, total)
        return total.astype(jnp.bfloat16)

    mine = info.at[x]
    mine[0:16] = stack((1.0 - second, second, 1.0 - second, second))
    mine[16:32] = stack((bias(-2), bias(-1), bias(2), bias(3)))
    for step in range(1, ROW):
        send(mine, mine, i_send, i_recv, (first + lax.rem(x + step, ROW), head))

    def spread(values):
        tall = jnp.concatenate([values, jnp.zeros((LANES - 16, run_len), jnp.float32)], axis=0)
        return jnp.transpose(tall).astype(jnp.bfloat16)

    def key_marks(slot):
        km[slot] = spread(info[slot, 0:16].astype(jnp.float32))

    def add_keys(state, q, marks, j, slot):
        top, total, acc = state
        k = kbuf[j, slot].reshape(run_len, HEAD_DIM)
        v = vbuf[j, slot].reshape(run_len, HEAD_DIM)
        if marks is not None:
            q = jnp.concatenate([q, marks], axis=1)
            k = jnp.concatenate([k, km[slot]], axis=1)
        scores = lax.dot_general(q, k, (((1,), (1,)), ((), ())), preferred_element_type=jnp.float32) * factor
        high = jnp.max(scores, axis=1, keepdims=True)
        new = high if top is None else jnp.maximum(top, high)
        weights = jnp.exp2(scores - new)
        part = jnp.sum(weights, axis=1, keepdims=True)
        mixed = jnp.dot(weights.astype(jnp.bfloat16), v, preferred_element_type=jnp.float32)
        if top is None:
            return new, part, mixed
        fade = jnp.exp2(top - new)
        return new, total * fade + part, acc * fade + mixed

    def load(j, run):
        at = lax.rem(j, 2)
        return top_s[at, run][:, 0:1], sum_s[at, run][:, 0:1], acc_s[at, run]

    def store(state, j, run):
        at = lax.rem(j, 2)
        top, total, acc = state
        top_s[at, run] = jnp.broadcast_to(top, (half, LANES))
        sum_s[at, run] = jnp.broadcast_to(total, (half, LANES))
        acc_s[at, run] = acc

    def marks_of(side, run, of):
        return qm[side, run, pl.ds(pl.multiple_of(of * half, half), half)]

    def my_queries(j, run):
        return queries_of(j, run)[...].reshape(half, HEAD_DIM)

    def step(j, run, slot, side):
        marks = None if side is None else marks_of(side, run, zl)
        store(add_keys(load(j, run), my_queries(j, run), marks, j, slot), j, run)

    def finish(acc, total, j, run):
        queries_like = (acc / total).astype(jnp.bfloat16).reshape(2, rows, HEAD_DIM)
        obuf[j, pl.ds(2 * run, 2)] = queries_like
        for c in range(2):
            peer = 2 * run + c

            @pl.when(peer != me)
            def _():
                send(obuf.at[j, peer], out.at[:, columns(me, j)], o_send.at[j], o_recv, device(peer))

            @pl.when(peer == me)
            def _():
                pltpu.make_async_copy(obuf.at[j, peer], out.at[:, columns(me, j)], o_recv).start()

    def finish_run(j, run):
        _, total, acc = load(j, run)
        finish(acc, total, j, run)

    def outer(j):
        @pl.when(j == 0)
        def _():
            wait(info.at[ROW], ih_recv)
            key_marks(ROW)

        for kind, _, buf in sources[:2]:
            wait(buf.at[j, ROW], h_recv.at[kind, j])
        wait(q_far.at[j], q_recv.at[j])
        far = q_far[j].reshape(half, HEAD_DIM)
        top, total, acc = add_keys((None, None, None), far, marks_of(zl, own_edge, 1 - zl), j, ROW)
        o_far[j] = (acc / total).astype(jnp.bfloat16).reshape(2, rows, HEAD_DIM)
        logs = jnp.broadcast_to(top + jnp.log2(total), (half, LANES))
        log_far[j] = jnp.transpose(logs)[0:8]
        send(o_far.at[j], o_back.at[j], p_send.at[j], p_recv.at[j], partner)
        send(log_far.at[j], log_back.at[j], l_send.at[j], l_recv.at[j], partner)
        state = add_keys(load(j, own_edge), my_queries(j, own_edge), marks_of(zl, own_edge, zl), j, ROW)
        finish(state[2], state[1], j, own_edge)

    def merge(j):
        wait(o_back.at[j], p_recv.at[j])
        wait(log_back.at[j], l_recv.at[j])
        top, total, acc = load(j, far_edge)
        logs = jnp.concatenate([log_back[j], jnp.zeros((LANES - 8, half), jnp.float32)], axis=0)
        log = jnp.transpose(logs)[:, 0:1]
        high = jnp.maximum(top, log)
        fade, other = jnp.exp2(top - high), jnp.exp2(log - high)
        back = o_back[j].reshape(half, HEAD_DIM).astype(jnp.float32)
        finish(acc * fade + back * other, total * fade + other, j, far_edge)

    def mirrored(index, flip):
        return index + flip * (last - 2 * index)

    def send_ahead(j, index):
        z_start(j, mirrored(index, 1 - zl))

        @pl.when(index == 1)
        def _():
            @pl.when(j + 1 < heads)
            def _():
                x_start(j + 1)

        @pl.when(index == last)
        def _():
            q_start(j)

    def ahead_first(index, carry):
        send_ahead(0, index)
        return carry

    lax.fori_loop(0, ROW, ahead_first, 0)

    def one_unit(t, carry):
        j = lax.div(t, ROW)
        index = lax.rem(t, ROW)
        run = mirrored(index, zl)

        @pl.when(j + 1 < heads)
        def _():
            send_ahead(j + 1, index)

        @pl.when(t == 0)
        def _():
            wait(info.at[pl.ds(0, ROW - 1)], i_recv)
            send(info.at[own_edge], info.at[ROW], ih_send, ih_recv, mate)
            for r in range(ROW):
                key_marks(r)
                marks = info[r, 16:32].astype(jnp.float32)
                qm[0, r] = spread(jnp.where(which < 2, marks, 0.0))
                qm[1, r] = spread(jnp.where(which >= 2, marks, 0.0))

        @pl.when(index == 0)
        def _():
            at = lax.rem(j, 2)
            top_s[at] = jnp.full((ROW, half, LANES), 4.0 * HIDE, jnp.float32)
            sum_s[at] = jnp.zeros((ROW, half, LANES), jnp.float32)
            acc_s[at] = jnp.zeros((ROW, half, HEAD_DIM), jnp.float32)

        @pl.when((index == 2) & (j > 0))
        def _():
            merge(j - 1)

        @pl.when(index == last)
        def _():
            outer(j)

        for kind, _, buf in sources[:2]:
            wait(unit(buf, j, run, 1 - zl), z_recv.at[kind, j, run])

        @pl.when(index == 0)
        def _():
            for kind, _, buf in sources[:2]:
                send(buf.at[j, run], buf.at[j, ROW], h_send.at[kind, j], h_recv.at[kind, j], mate)

        step(j, run, run, None)

        @pl.when(run < last)
        def _():
            step(j, run + 1, run, 0)

        @pl.when(run > 0)
        def _():
            step(j, run - 1, run, 1)

        @pl.when(index >= 2)
        def _():
            finish_run(j, mirrored(index - 1, zl))

        return carry

    lax.fori_loop(0, heads * ROW, one_unit, 0)
    merge(heads - 1)

    wait(out, o_recv)
    wait(info.at[pl.ds(0, ROW - 1)], i_send)
    wait(info.at[0], ih_send)

    def drain(j, carry):
        for kind, _, buf in sources:
            wait(qbuf.at[j, pl.ds(0, PEERS - 1)], x_send.at[kind, j])
            if kind < 2:
                wait(qbuf.at[j, pl.ds(0, 2)], d_send.at[kind, j])
                wait(buf.at[j, ROW], h_send.at[kind, j])
                for run in range(ROW):
                    @pl.when(run != x)
                    def _():
                        wait(unit(buf, j, run, zl), z_send.at[kind, j, run])
        wait(qbuf.at[j, pl.ds(0, PEERS - 1)], o_send.at[j])
        wait(q_far.at[j], q_send.at[j])
        wait(o_far.at[j], p_send.at[j])
        wait(log_far.at[j], l_send.at[j])
        return carry

    lax.fori_loop(0, heads, drain, 0)


def local(queries, key_input, value_input, token_order, tile_mask):
    rows, width = queries.shape
    heads = width // HEAD_DIM // PEERS
    runs = lax.axis_size("blk")
    run_len = 4 * rows
    half = 2 * rows
    bf16, f32 = jnp.bfloat16, jnp.float32
    dma = pltpu.SemaphoreType.DMA
    hbm = pl.BlockSpec(memory_space=pl.ANY)
    vmem = pl.BlockSpec(memory_space=pltpu.VMEM)
    flops = 4 * heads * ROW * half * 3 * run_len * HEAD_DIM
    return pl.pallas_call(
        functools.partial(kernel, heads, runs),
        out_shape=jax.ShapeDtypeStruct(queries.shape, queries.dtype),
        in_specs=[hbm, hbm, hbm, vmem, vmem],
        out_specs=hbm,
        scratch_shapes=[
            pltpu.VMEM((heads, ROW + 1, 4, rows, HEAD_DIM), bf16),
            pltpu.VMEM((heads, ROW + 1, 4, rows, HEAD_DIM), bf16),
            pltpu.VMEM((heads, PEERS, rows, HEAD_DIM), bf16),
            pltpu.VMEM((heads, PEERS, rows, HEAD_DIM), bf16),
            pltpu.VMEM((heads, 2, rows, HEAD_DIM), bf16),
            pltpu.VMEM((heads, 2, rows, HEAD_DIM), bf16),
            pltpu.VMEM((heads, 2, rows, HEAD_DIM), bf16),
            pltpu.VMEM((heads, 8, half), f32),
            pltpu.VMEM((heads, 8, half), f32),
            pltpu.VMEM((ROW + 1, 32, run_len), bf16),
            pltpu.VMEM((ROW + 1, run_len, LANES), bf16),
            pltpu.VMEM((2, ROW, run_len, LANES), bf16),
            pltpu.VMEM((2, ROW, half, LANES), f32),
            pltpu.VMEM((2, ROW, half, LANES), f32),
            pltpu.VMEM((2, ROW, half, HEAD_DIM), f32),
            dma((3, heads, ROW)), dma((3, heads)),
            dma((2, heads, ROW)), dma((2, heads, ROW)), dma((2, heads)),
            dma((2, heads)), dma((2, heads)),
            dma, dma((heads,)),
            dma, dma, dma, dma,
            dma((heads,)), dma((heads,)),
            dma((heads,)), dma((heads,)),
            dma((heads,)), dma((heads,)),
        ],
        compiler_params=pltpu.CompilerParams(
            collective_id=0, has_side_effects=True, vmem_limit_bytes=56 * 1024 * 1024
        ),
        cost_estimate=pl.CostEstimate(
            flops=flops, bytes_accessed=8 * rows * width, transcendentals=flops // (4 * HEAD_DIM)
        ),
    )(queries, key_input, value_input, token_order.reshape(1, run_len), tile_mask)


def solution(mesh):
    in_specs = (
        P(("blk", "head"), None),
        P(("blk", "head"), None),
        P(("blk", "head"), None),
        P("blk"),
        P("blk", None),
    )
    out_specs = P(("blk", "head"), None)
    return jax.shard_map(local, mesh=mesh, in_specs=in_specs, out_specs=out_specs, check_vma=False)
```

```python
import functools
import math

import jax
import jax.numpy as jnp
from jax import lax
from jax.experimental import pallas as pl
from jax.experimental.pallas import tpu as pltpu
from jax.sharding import PartitionSpec as P

HEAD_DIM = 128
ROW = 4
PEERS = 2 * ROW
LANES = 128
HIDE = -(2.0**100)
MESH = pl.DeviceIdType.MESH


def kernel(
    heads, runs,
    q_in, k_in, v_in, order_ref, mask_ref,
    out,
    kbuf, vbuf, qbuf, obuf, q_far, o_far, o_back, log_far, log_back, info, km, qm, top_s, sum_s, acc_s,
    x_recv, x_send, z_recv, z_send, d_send, h_recv, h_send, o_recv, o_send, i_recv, i_send, ih_recv, ih_send,
    q_recv, q_send, p_recv, p_send, l_recv, l_send,
):
    rows = q_in.shape[0]
    run_len = 4 * rows
    half = 2 * rows
    factor = math.log2(math.e) / math.sqrt(HEAD_DIM)
    last = ROW - 1

    blk = lax.axis_index("blk")
    head = lax.axis_index("head")
    x = lax.rem(blk, ROW)
    first = blk - x
    zl = lax.div(head, 2)
    core = lax.rem(head, 2)
    me = 2 * x + core
    across = 2 * (1 - zl)
    partner = (blk, across + core)
    mate = (lax.rem(blk + runs + (2 * zl - 1) * ROW, runs), across + core)
    own_edge = last * zl
    far_edge = last * (1 - zl)

    def device(peer):
        return (first + lax.div(peer, 2), 2 * zl + lax.rem(peer, 2))

    def peer_at(step):
        return lax.rem(me + step, PEERS)

    barrier = pltpu.get_barrier_semaphore()
    greet = [device(peer_at(step)) for step in range(1, PEERS)]
    greet += [partner, (blk, across + 1 - core), mate]
    for to in greet:
        pl.semaphore_signal(barrier, inc=1, device_id=to, device_id_type=MESH)

    order = (order_ref[...].reshape(1, run_len) - blk * run_len).astype(jnp.float32)
    order = jnp.transpose(jnp.broadcast_to(order, (LANES, run_len)))[half:]
    lane = lax.broadcasted_iota(jnp.int32, (half, LANES), 1).astype(jnp.float32)
    second = jnp.concatenate(
        [
            jnp.sum(jnp.where(order == lane + LANES * g, 1.0, 0.0), axis=0, keepdims=True)
            for g in range(run_len // LANES)
        ],
        axis=1,
    )
    seen = mask_ref[...].astype(jnp.float32)
    mask_lane = lax.broadcasted_iota(jnp.int32, seen.shape, 1)

    def bias(offset):
        column = jnp.sum(jnp.where(mask_lane == 2 * blk + offset, seen, 0.0), axis=1, keepdims=True)
        return HIDE * (1.0 - (column[0:1] + second * (column[1:2] - column[0:1])))

    which = lax.broadcasted_iota(jnp.int32, (16, run_len), 0)
    log_row = lax.broadcasted_iota(jnp.int32, (8, LANES), 0)

    def stack(parts):
        total = jnp.zeros((16, run_len), jnp.float32)
        for index, part in enumerate(parts):
            total = jnp.where(which == index, part, total)
        return total.astype(jnp.bfloat16)

    mine = info.at[x]
    mine[0:16] = stack((1.0 - second, second, 1.0 - second, second))
    mine[16:32] = stack((bias(-2), bias(-1), bias(2), bias(3)))
    pl.semaphore_wait(barrier, len(greet))

    def columns(peer, j):
        return pl.ds(pl.multiple_of((heads * peer + j) * HEAD_DIM, HEAD_DIM), HEAD_DIM)

    def send(src, dst, send_sem, recv_sem, to):
        pltpu.make_async_remote_copy(
            src_ref=src, dst_ref=dst, send_sem=send_sem, recv_sem=recv_sem, device_id=to, device_id_type=MESH
        ).start()

    def wait(like, sem):
        pltpu.make_async_copy(like, like, sem).wait()

    sources = ((0, k_in, kbuf), (1, v_in, vbuf), (2, q_in, qbuf))

    def direct_start(j):
        for kind, source, buf in sources[:2]:
            for c in range(2):
                send(
                    source.at[:, columns(2 * x + c, j)], buf.at[j, x, head],
                    d_send.at[kind, j], z_recv.at[kind, j, x], (blk, across + c),
                )

    def x_start(j):
        for kind, source, buf in sources:
            place = qbuf.at[j, me] if kind == 2 else buf.at[j, x, head]
            pltpu.make_async_copy(source.at[:, columns(me, j)], place, x_recv.at[kind, j, x]).start()
            for step in range(1, PEERS):
                peer = peer_at(step)
                send(
                    source.at[:, columns(peer, j)], place,
                    x_send.at[kind, j], x_recv.at[kind, j, x], device(peer),
                )

    def unit(buf, j, run, side):
        return buf.at[j, run, pl.ds(2 * side, 2)]

    def halo_start(kind, buf, j, side):
        send(unit(buf, j, own_edge, side), unit(buf, j, ROW, side), h_send.at[kind, j], h_recv.at[kind, j], mate)

    def z_start(j, run):
        for kind, _, buf in sources[:2]:
            wait(unit(buf, j, run, zl), x_recv.at[kind, j, run])

            @pl.when((run != x) | (j == heads - 1))
            def _():
                send(
                    unit(buf, j, run, zl), unit(buf, j, run, zl),
                    z_send.at[kind, j], z_recv.at[kind, j, run], partner,
                )

            @pl.when(run == own_edge)
            def _():
                halo_start(kind, buf, j, zl)

    def queries_of(j, run):
        return qbuf.at[j, pl.ds(2 * run, 2)]

    def q_start(j):
        for run in range(ROW):
            wait(queries_of(j, run), x_recv.at[2, j, run])
        send(queries_of(j, far_edge), q_far.at[j], q_send.at[j], q_recv.at[j], partner)

    direct_start(0)
    x_start(0)
    for j in range(1, heads - 1):
        direct_start(j)

    for step in range(1, ROW):
        send(mine, mine, i_send, i_recv, (first + lax.rem(x + step, ROW), head))

    def spread(values):
        tall = jnp.concatenate([values, jnp.zeros((LANES - 16, run_len), jnp.float32)], axis=0)
        return jnp.transpose(tall).astype(jnp.bfloat16)

    def key_marks(slot):
        km[slot] = spread(info[slot, 0:16].astype(jnp.float32))

    def add_keys(state, q, marks, j, slot):
        top, total, acc = state
        k = kbuf[j, slot].reshape(run_len, HEAD_DIM)
        v = vbuf[j, slot].reshape(run_len, HEAD_DIM)
        if marks is not None:
            q = jnp.concatenate([q, marks], axis=1)
            k = jnp.concatenate([k, km[slot]], axis=1)
        scores = lax.dot_general(k, q, (((1,), (1,)), ((), ())), preferred_element_type=jnp.float32) * factor
        high = jnp.max(scores, axis=0, keepdims=True)
        new = high if top is None else jnp.maximum(top, high)
        weights = jnp.exp2(scores - new)
        part = jnp.sum(weights, axis=0, keepdims=True)
        mixed = lax.dot_general(
            v, weights.astype(jnp.bfloat16), (((0,), (0,)), ((), ())), preferred_element_type=jnp.float32
        )
        if top is None:
            return new, part, mixed
        fade = jnp.exp2(top - new)
        return new, total * fade + part, acc * fade + mixed

    def load(j, run):
        at = lax.rem(j, 2)
        return top_s[at, run][0:1], sum_s[at, run][0:1], acc_s[at, run]

    def store(state, j, run):
        at = lax.rem(j, 2)
        top, total, acc = state
        top_s[at, run] = jnp.broadcast_to(top, (8, half))
        sum_s[at, run] = jnp.broadcast_to(total, (8, half))
        acc_s[at, run] = acc

    def marks_of(side, run, of):
        return qm[side, run, pl.ds(pl.multiple_of(of * half, half), half)]

    def my_queries(j, run):
        return queries_of(j, run)[...].reshape(half, HEAD_DIM)

    def steps(j, slot, pairs):
        states = []
        for run, side in pairs:
            marks = None if side is None else marks_of(side, run, zl)
            states.append(add_keys(load(j, run), my_queries(j, run), marks, j, slot))
        for (run, _), state in zip(pairs, states):
            store(state, j, run)

    def finish(acc, total, j, run):
        rows_first = jnp.transpose(acc / total).astype(jnp.bfloat16)
        obuf[j, pl.ds(2 * run, 2)] = rows_first.reshape(2, rows, HEAD_DIM)
        for c in range(2):
            peer = 2 * run + c

            @pl.when(peer != me)
            def _():
                send(obuf.at[j, peer], out.at[:, columns(me, j)], o_send.at[j], o_recv, device(peer))

            @pl.when(peer == me)
            def _():
                pltpu.make_async_copy(obuf.at[j, peer], out.at[:, columns(me, j)], o_recv).start()

    def finish_run(j, run):
        _, total, acc = load(j, run)
        finish(acc, total, j, run)

    def outer(j):
        @pl.when(j == 0)
        def _():
            wait(info.at[ROW], ih_recv)
            key_marks(ROW)

        for kind, _, buf in sources[:2]:
            wait(buf.at[j, ROW], h_recv.at[kind, j])
        wait(q_far.at[j], q_recv.at[j])
        far = q_far[j].reshape(half, HEAD_DIM)
        top, total, acc = add_keys((None, None, None), far, marks_of(zl, own_edge, 1 - zl), j, ROW)
        state = add_keys(load(j, own_edge), my_queries(j, own_edge), marks_of(zl, own_edge, zl), j, ROW)
        o_far[j] = (acc / total).astype(jnp.bfloat16)
        logs = top + jnp.log2(total)
        packed = jnp.zeros((8, LANES), jnp.float32)
        for g in range(half // LANES):
            packed = jnp.where(log_row == g, logs[:, g * LANES : (g + 1) * LANES], packed)
        log_far[j] = packed
        send(o_far.at[j], o_back.at[j], p_send.at[j], p_recv.at[j], partner)
        send(log_far.at[j], log_back.at[j], l_send.at[j], l_recv.at[j], partner)
        finish(state[2], state[1], j, own_edge)

    def merge(j):
        wait(o_back.at[j], p_recv.at[j])
        wait(log_back.at[j], l_recv.at[j])
        top, total, acc = load(j, far_edge)
        logs = log_back[j]
        log = jnp.concatenate([logs[g : g + 1] for g in range(half // LANES)], axis=1)
        high = jnp.maximum(top, log)
        fade, other = jnp.exp2(top - high), jnp.exp2(log - high)
        finish(acc * fade + o_back[j].astype(jnp.float32) * other, total * fade + other, j, far_edge)

    def mirrored(index, flip):
        return index + flip * (last - 2 * index)

    def send_ahead(j, index):
        z_start(j, mirrored(index, 1 - zl))

        @pl.when(index == 1)
        def _():
            @pl.when(j + 1 < heads)
            def _():
                x_start(j + 1)

        @pl.when(index == last)
        def _():
            q_start(j)

    def ahead_first(index, carry):
        send_ahead(0, index)
        return carry

    lax.fori_loop(0, ROW, ahead_first, 0)

    def drain_early(j, direct):
        for kind, _, buf in sources:
            wait(qbuf.at[j, pl.ds(0, PEERS - 1)], x_send.at[kind, j])
            if kind < 2:
                if direct:
                    wait(qbuf.at[j, pl.ds(0, 2)], d_send.at[kind, j])
                wait(buf.at[j, pl.ds(0, ROW - direct), pl.ds(0, 2)], z_send.at[kind, j])
                wait(buf.at[j, ROW], h_send.at[kind, j])
        wait(q_far.at[j], q_send.at[j])

    def drain_late(j):
        wait(qbuf.at[j, pl.ds(0, PEERS - 1)], o_send.at[j])
        wait(o_far.at[j], p_send.at[j])
        wait(log_far.at[j], l_send.at[j])

    def one_unit(t, carry):
        j = lax.div(t, ROW)
        index = lax.rem(t, ROW)
        run = mirrored(index, zl)

        @pl.when(j + 1 < heads)
        def _():
            send_ahead(j + 1, index)

        @pl.when(t == 0)
        def _():
            wait(info.at[pl.ds(0, ROW - 1)], i_recv)
            send(info.at[own_edge], info.at[ROW], ih_send, ih_recv, mate)
            for r in range(ROW):
                key_marks(r)
                marks = info[r, 16:32].astype(jnp.float32)
                qm[0, r] = spread(jnp.where(which < 2, marks, 0.0))
                qm[1, r] = spread(jnp.where(which >= 2, marks, 0.0))

        @pl.when(index == 0)
        def _():
            at = lax.rem(j, 2)
            top_s[at] = jnp.full((ROW, 8, half), 4.0 * HIDE, jnp.float32)
            sum_s[at] = jnp.zeros((ROW, 8, half), jnp.float32)
            acc_s[at] = jnp.zeros((ROW, HEAD_DIM, half), jnp.float32)

        @pl.when((index == 1) & (j > 0))
        def _():
            drain_early(j - 1, 1)

        @pl.when((index == 1) & (j > 1))
        def _():
            drain_late(j - 2)

        @pl.when((index == 2) & (j > 0))
        def _():
            merge(j - 1)

        @pl.when(index == 2)
        def _():
            outer(j)

        for kind, _, buf in sources[:2]:
            wait(unit(buf, j, run, 1 - zl), z_recv.at[kind, j, run])

        @pl.when(index == 0)
        def _():
            for kind, _, buf in sources[:2]:
                halo_start(kind, buf, j, 1 - zl)

        ahead, behind = (run + 1 - 2 * zl, zl), (run - 1 + 2 * zl, 1 - zl)

        @pl.when(index == 0)
        def _():
            steps(j, run, [ahead, (run, None)])

        @pl.when((index > 0) & (index < last))
        def _():
            steps(j, run, [behind, ahead, (run, None)])

        @pl.when(index == last)
        def _():
            steps(j, run, [behind, (run, None)])

        @pl.when(index >= 2)
        def _():
            finish_run(j, mirrored(index - 1, zl))

        return carry

    lax.fori_loop(0, heads * ROW, one_unit, 0)
    drain_early(heads - 1, 0)
    if heads > 1:
        drain_late(heads - 2)
    wait(info.at[pl.ds(0, ROW - 1)], i_send)
    wait(info.at[0], ih_send)
    merge(heads - 1)
    drain_late(heads - 1)
    wait(out, o_recv)


def local(queries, key_input, value_input, token_order, tile_mask):
    rows, width = queries.shape
    heads = width // HEAD_DIM // PEERS
    runs = lax.axis_size("blk")
    run_len = 4 * rows
    half = 2 * rows
    bf16, f32 = jnp.bfloat16, jnp.float32
    dma = pltpu.SemaphoreType.DMA
    hbm = pl.BlockSpec(memory_space=pl.ANY)
    vmem = pl.BlockSpec(memory_space=pltpu.VMEM)
    flops = 4 * heads * ROW * half * 3 * run_len * HEAD_DIM
    return pl.pallas_call(
        functools.partial(kernel, heads, runs),
        out_shape=jax.ShapeDtypeStruct(queries.shape, queries.dtype),
        in_specs=[hbm, hbm, hbm, vmem, vmem],
        out_specs=hbm,
        scratch_shapes=[
            pltpu.VMEM((heads, ROW + 1, 4, rows, HEAD_DIM), bf16),
            pltpu.VMEM((heads, ROW + 1, 4, rows, HEAD_DIM), bf16),
            pltpu.VMEM((heads, PEERS, rows, HEAD_DIM), bf16),
            pltpu.VMEM((heads, PEERS, rows, HEAD_DIM), bf16),
            pltpu.VMEM((heads, 2, rows, HEAD_DIM), bf16),
            pltpu.VMEM((heads, HEAD_DIM, half), bf16),
            pltpu.VMEM((heads, HEAD_DIM, half), bf16),
            pltpu.VMEM((heads, 8, LANES), f32),
            pltpu.VMEM((heads, 8, LANES), f32),
            pltpu.VMEM((ROW + 1, 32, run_len), bf16),
            pltpu.VMEM((ROW + 1, run_len, LANES), bf16),
            pltpu.VMEM((2, ROW, run_len, LANES), bf16),
            pltpu.VMEM((2, ROW, 8, half), f32),
            pltpu.VMEM((2, ROW, 8, half), f32),
            pltpu.VMEM((2, ROW, HEAD_DIM, half), f32),
            dma((3, heads, ROW)), dma((3, heads)),
            dma((2, heads, ROW)), dma((2, heads)), dma((2, heads)),
            dma((2, heads)), dma((2, heads)),
            dma, dma((heads,)),
            dma, dma, dma, dma,
            dma((heads,)), dma((heads,)),
            dma((heads,)), dma((heads,)),
            dma((heads,)), dma((heads,)),
        ],
        compiler_params=pltpu.CompilerParams(
            collective_id=0, has_side_effects=True, vmem_limit_bytes=56 * 1024 * 1024
        ),
        cost_estimate=pl.CostEstimate(
            flops=flops, bytes_accessed=8 * rows * width, transcendentals=flops // (4 * HEAD_DIM)
        ),
    )(queries, key_input, value_input, token_order, tile_mask)


def solution(mesh):
    in_specs = (
        P(("blk", "head"), None),
        P(("blk", "head"), None),
        P(("blk", "head"), None),
        P("blk"),
        P("blk", None),
    )
    out_specs = P(("blk", "head"), None)
    return jax.shard_map(local, mesh=mesh, in_specs=in_specs, out_specs=out_specs, check_vma=False)
```

```python
import functools
import math

import jax
import jax.numpy as jnp
from jax import lax
from jax.experimental import pallas as pl
from jax.experimental.pallas import tpu as pltpu
from jax.sharding import PartitionSpec as P

HEAD_DIM = 128
ROW = 4
PEERS = 2 * ROW
LANES = 128
HIDE = -(2.0**100)
MESH = pl.DeviceIdType.MESH


def kernel(
    heads, runs,
    q_in, k_in, v_in, order_in, mask_in,
    out,
    kbuf, vbuf, qbuf, obuf, q_far, o_far, o_back, log_far, log_back, info, km, qm, top_s, sum_s, acc_s,
    x_recv, x_send, z_recv, z_send, d_send, h_recv, h_send, o_recv, o_send, i_recv, i_send, ih_recv, ih_send,
    q_recv, q_send, p_recv, p_send, l_recv, l_send, order_ref, mask_ref, tile_sem,
):
    rows = q_in.shape[0]
    run_len = 4 * rows
    half = 2 * rows
    factor = math.log2(math.e) / math.sqrt(HEAD_DIM)
    last = ROW - 1

    blk = lax.axis_index("blk")
    head = lax.axis_index("head")
    x = lax.rem(blk, ROW)
    first = blk - x
    zl = lax.div(head, 2)
    core = lax.rem(head, 2)
    me = 2 * x + core
    across = 2 * (1 - zl)
    partner = (blk, across + core)
    mate = (lax.rem(blk + runs + (2 * zl - 1) * ROW, runs), across + core)
    own_edge = last * zl
    far_edge = last * (1 - zl)

    def device(peer):
        return (first + lax.div(peer, 2), 2 * zl + lax.rem(peer, 2))

    def peer_at(step):
        return lax.rem(me + step, PEERS)

    barrier = pltpu.get_barrier_semaphore()
    greet = [device(peer_at(step)) for step in range(1, PEERS)]
    greet += [partner, (blk, across + 1 - core), mate]
    for to in greet:
        pl.semaphore_signal(barrier, inc=1, device_id=to, device_id_type=MESH)

    order_copy = pltpu.make_async_copy(order_in, order_ref, tile_sem.at[0])
    mask_copy = pltpu.make_async_copy(mask_in, mask_ref, tile_sem.at[1])
    order_copy.start()
    mask_copy.start()
    order_copy.wait()
    mask_copy.wait()

    order = (order_ref[...].reshape(1, run_len) - blk * run_len).astype(jnp.float32)
    order = jnp.transpose(jnp.broadcast_to(order, (LANES, run_len)))[half:]
    lane = lax.broadcasted_iota(jnp.int32, (half, LANES), 1).astype(jnp.float32)
    second = jnp.concatenate(
        [
            jnp.sum(jnp.where(order == lane + LANES * g, 1.0, 0.0), axis=0, keepdims=True)
            for g in range(run_len // LANES)
        ],
        axis=1,
    )
    seen = mask_ref[...].astype(jnp.float32)
    mask_lane = lax.broadcasted_iota(jnp.int32, seen.shape, 1)

    def bias(offset):
        column = jnp.sum(jnp.where(mask_lane == 2 * blk + offset, seen, 0.0), axis=1, keepdims=True)
        return HIDE * (1.0 - (column[0:1] + second * (column[1:2] - column[0:1])))

    which = lax.broadcasted_iota(jnp.int32, (16, run_len), 0)
    log_row = lax.broadcasted_iota(jnp.int32, (8, LANES), 0)

    def stack(parts):
        total = jnp.zeros((16, run_len), jnp.float32)
        for index, part in enumerate(parts):
            total = jnp.where(which == index, part, total)
        return total.astype(jnp.bfloat16)

    mine = info.at[x]
    mine[0:16] = stack((1.0 - second, second, 1.0 - second, second))
    mine[16:32] = stack((bias(-2), bias(-1), bias(2), bias(3)))
    pl.semaphore_wait(barrier, len(greet))

    def columns(peer, j):
        return pl.ds(pl.multiple_of((heads * peer + j) * HEAD_DIM, HEAD_DIM), HEAD_DIM)

    def send(src, dst, send_sem, recv_sem, to):
        pltpu.make_async_remote_copy(
            src_ref=src, dst_ref=dst, send_sem=send_sem, recv_sem=recv_sem, device_id=to, device_id_type=MESH
        ).start()

    def wait(like, sem):
        pltpu.make_async_copy(like, like, sem).wait()

    sources = ((0, k_in, kbuf), (1, v_in, vbuf), (2, q_in, qbuf))

    def direct_start(j):
        for kind, source, buf in sources[:2]:
            for c in range(2):
                send(
                    source.at[:, columns(2 * x + c, j)], buf.at[j, x, head],
                    d_send.at[kind, j], z_recv.at[kind, j, x], (blk, across + c),
                )

    def x_start(j):
        for kind, source, buf in sources:
            place = qbuf.at[j, me] if kind == 2 else buf.at[j, x, head]
            pltpu.make_async_copy(source.at[:, columns(me, j)], place, x_recv.at[kind, j, x]).start()
            for step in range(1, PEERS):
                peer = peer_at(step)
                send(
                    source.at[:, columns(peer, j)], place,
                    x_send.at[kind, j], x_recv.at[kind, j, x], device(peer),
                )

    def unit(buf, j, run, side):
        return buf.at[j, run, pl.ds(2 * side, 2)]

    def halo_start(kind, buf, j, side):
        send(unit(buf, j, own_edge, side), unit(buf, j, ROW, side), h_send.at[kind, j], h_recv.at[kind, j], mate)

    def z_start(j, run):
        for kind, _, buf in sources[:2]:
            @pl.when(run != own_edge)
            def _():
                wait(unit(buf, j, run, zl), x_recv.at[kind, j, run])

            @pl.when((run != x) | (j == heads - 1))
            def _():
                send(
                    unit(buf, j, run, zl), unit(buf, j, run, zl),
                    z_send.at[kind, j], z_recv.at[kind, j, run], partner,
                )

    def queries_of(j, run):
        return qbuf.at[j, pl.ds(2 * run, 2)]

    def q_start(j):
        for run in range(ROW):
            wait(queries_of(j, run), x_recv.at[2, j, run])
        send(queries_of(j, far_edge), q_far.at[j], q_send.at[j], q_recv.at[j], partner)

    direct_start(0)
    x_start(0)
    for j in range(1, heads - 1):
        direct_start(j)

    for step in range(1, ROW):
        send(mine, mine, i_send, i_recv, (first + lax.rem(x + step, ROW), head))

    def spread(values):
        tall = jnp.concatenate([values, jnp.zeros((LANES - 16, run_len), jnp.float32)], axis=0)
        return jnp.transpose(tall).astype(jnp.bfloat16)

    def key_marks(slot):
        km[slot] = spread(info[slot, 0:16].astype(jnp.float32))

    def add_keys(state, q, marks, j, slot):
        top, total, acc = state
        k = kbuf[j, slot].reshape(run_len, HEAD_DIM)
        v = vbuf[j, slot].reshape(run_len, HEAD_DIM)
        if marks is not None:
            q = jnp.concatenate([q, marks], axis=1)
            k = jnp.concatenate([k, km[slot]], axis=1)
        scores = lax.dot_general(k, q, (((1,), (1,)), ((), ())), preferred_element_type=jnp.float32) * factor
        high = jnp.max(scores, axis=0, keepdims=True)
        new = high if top is None else jnp.maximum(top, high)
        weights = jnp.exp2(scores - new)
        part = jnp.sum(weights, axis=0, keepdims=True)
        mixed = lax.dot_general(
            v, weights.astype(jnp.bfloat16), (((0,), (0,)), ((), ())), preferred_element_type=jnp.float32
        )
        if top is None:
            return new, part, mixed
        fade = jnp.exp2(top - new)
        return new, total * fade + part, acc * fade + mixed

    def load(j, run):
        at = lax.rem(j, 2)
        return top_s[at, run][0:1], sum_s[at, run][0:1], acc_s[at, run]

    def store(state, j, run):
        at = lax.rem(j, 2)
        top, total, acc = state
        top_s[at, run] = jnp.broadcast_to(top, (8, half))
        sum_s[at, run] = jnp.broadcast_to(total, (8, half))
        acc_s[at, run] = acc

    def marks_of(side, run, of):
        return qm[side, run, pl.ds(pl.multiple_of(of * half, half), half)]

    def my_queries(j, run):
        return queries_of(j, run)[...].reshape(half, HEAD_DIM)

    def steps(j, slot, pairs):
        states = []
        for run, side in pairs:
            marks = None if side is None else marks_of(side, run, zl)
            states.append(add_keys(load(j, run), my_queries(j, run), marks, j, slot))
        for (run, _), state in zip(pairs, states):
            store(state, j, run)

    def finish(acc, total, j, run):
        rows_first = jnp.transpose(acc / total).astype(jnp.bfloat16)
        obuf[j, pl.ds(2 * run, 2)] = rows_first.reshape(2, rows, HEAD_DIM)
        for c in range(2):
            peer = 2 * run + c

            @pl.when(peer != me)
            def _():
                send(obuf.at[j, peer], out.at[:, columns(me, j)], o_send.at[j], o_recv, device(peer))

            @pl.when(peer == me)
            def _():
                pltpu.make_async_copy(obuf.at[j, peer], out.at[:, columns(me, j)], o_recv).start()

    def finish_run(j, run):
        _, total, acc = load(j, run)
        finish(acc, total, j, run)

    def outer(j):
        @pl.when(j == 0)
        def _():
            wait(info.at[ROW], ih_recv)
            key_marks(ROW)

        for kind, _, buf in sources[:2]:
            wait(buf.at[j, ROW], h_recv.at[kind, j])
        wait(q_far.at[j], q_recv.at[j])
        far = q_far[j].reshape(half, HEAD_DIM)
        top, total, acc = add_keys((None, None, None), far, marks_of(zl, own_edge, 1 - zl), j, ROW)
        state = add_keys(load(j, own_edge), my_queries(j, own_edge), marks_of(zl, own_edge, zl), j, ROW)
        o_far[j] = (acc / total).astype(jnp.bfloat16)
        logs = top + jnp.log2(total)
        packed = jnp.zeros((8, LANES), jnp.float32)
        for g in range(half // LANES):
            packed = jnp.where(log_row == g, logs[:, g * LANES : (g + 1) * LANES], packed)
        log_far[j] = packed
        send(o_far.at[j], o_back.at[j], p_send.at[j], p_recv.at[j], partner)
        send(log_far.at[j], log_back.at[j], l_send.at[j], l_recv.at[j], partner)
        finish(state[2], state[1], j, own_edge)

    def merge(j):
        wait(o_back.at[j], p_recv.at[j])
        wait(log_back.at[j], l_recv.at[j])
        top, total, acc = load(j, far_edge)
        logs = log_back[j]
        log = jnp.concatenate([logs[g : g + 1] for g in range(half // LANES)], axis=1)
        high = jnp.maximum(top, log)
        fade, other = jnp.exp2(top - high), jnp.exp2(log - high)
        finish(acc * fade + o_back[j].astype(jnp.float32) * other, total * fade + other, j, far_edge)

    def mirrored(index, flip):
        return index + flip * (last - 2 * index)

    def send_ahead(j, index):
        @pl.when(index == 0)
        def _():
            for kind, _, buf in sources[:2]:
                wait(unit(buf, j, own_edge, zl), x_recv.at[kind, j, own_edge])
                halo_start(kind, buf, j, zl)

        z_start(j, mirrored(index, 1 - zl))

        @pl.when(index == 0)
        def _():
            q_start(j)

            @pl.when(j + 1 < heads)
            def _():
                x_start(j + 1)

    def ahead_first(index, carry):
        send_ahead(0, index)
        return carry

    lax.fori_loop(0, ROW, ahead_first, 0)

    def drain_early(j, direct):
        for kind, _, buf in sources:
            wait(qbuf.at[j, pl.ds(0, PEERS - 1)], x_send.at[kind, j])
            if kind < 2:
                if direct:
                    wait(qbuf.at[j, pl.ds(0, 2)], d_send.at[kind, j])
                wait(buf.at[j, pl.ds(0, ROW - direct), pl.ds(0, 2)], z_send.at[kind, j])
                wait(buf.at[j, ROW], h_send.at[kind, j])
        wait(q_far.at[j], q_send.at[j])

    def drain_late(j):
        wait(qbuf.at[j, pl.ds(0, PEERS - 1)], o_send.at[j])
        wait(o_far.at[j], p_send.at[j])
        wait(log_far.at[j], l_send.at[j])

    def one_unit(t, carry):
        j = lax.div(t, ROW)
        index = lax.rem(t, ROW)
        run = mirrored(index, zl)

        @pl.when(j + 1 < heads)
        def _():
            send_ahead(j + 1, index)

        @pl.when(t == 0)
        def _():
            wait(info.at[pl.ds(0, ROW - 1)], i_recv)
            send(info.at[own_edge], info.at[ROW], ih_send, ih_recv, mate)
            for r in range(ROW):
                key_marks(r)
                marks = info[r, 16:32].astype(jnp.float32)
                qm[0, r] = spread(jnp.where(which < 2, marks, 0.0))
                qm[1, r] = spread(jnp.where(which >= 2, marks, 0.0))

        @pl.when(index == 0)
        def _():
            at = lax.rem(j, 2)
            top_s[at] = jnp.full((ROW, 8, half), 4.0 * HIDE, jnp.float32)
            sum_s[at] = jnp.zeros((ROW, 8, half), jnp.float32)
            acc_s[at] = jnp.zeros((ROW, HEAD_DIM, half), jnp.float32)

        @pl.when((index == 1) & (j > 0))
        def _():
            drain_early(j - 1, 1)

        @pl.when((index == 1) & (j > 1))
        def _():
            drain_late(j - 2)

        @pl.when((index == 2) & (j > 0))
        def _():
            merge(j - 1)

        @pl.when(index == 2)
        def _():
            outer(j)

        for kind, _, buf in sources[:2]:
            wait(unit(buf, j, run, 1 - zl), z_recv.at[kind, j, run])

        @pl.when(index == 0)
        def _():
            for kind, _, buf in sources[:2]:
                halo_start(kind, buf, j, 1 - zl)

        ahead, behind = (run + 1 - 2 * zl, zl), (run - 1 + 2 * zl, 1 - zl)

        @pl.when(index == 0)
        def _():
            steps(j, run, [ahead, (run, None)])

        @pl.when((index > 0) & (index < last))
        def _():
            steps(j, run, [behind, ahead, (run, None)])

        @pl.when(index == last)
        def _():
            steps(j, run, [behind, (run, None)])

        @pl.when(index >= 2)
        def _():
            finish_run(j, mirrored(index - 1, zl))

        return carry

    lax.fori_loop(0, heads * ROW, one_unit, 0)
    drain_early(heads - 1, 0)
    if heads > 1:
        drain_late(heads - 2)
    wait(info.at[pl.ds(0, ROW - 1)], i_send)
    wait(info.at[0], ih_send)
    merge(heads - 1)
    drain_late(heads - 1)
    wait(out, o_recv)


def local(queries, key_input, value_input, token_order, tile_mask):
    rows, width = queries.shape
    heads = width // HEAD_DIM // PEERS
    runs = lax.axis_size("blk")
    run_len = 4 * rows
    half = 2 * rows
    bf16, f32 = jnp.bfloat16, jnp.float32
    dma = pltpu.SemaphoreType.DMA
    hbm = pl.BlockSpec(memory_space=pl.ANY)
    vmem = pl.BlockSpec(memory_space=pltpu.VMEM)
    flops = 4 * heads * ROW * half * 3 * run_len * HEAD_DIM
    return pl.pallas_call(
        functools.partial(kernel, heads, runs),
        out_shape=pltpu.VMEM(queries.shape, queries.dtype),
        in_specs=[hbm] * 5,
        out_specs=vmem,
        scratch_shapes=[
            pltpu.VMEM((heads, ROW + 1, 4, rows, HEAD_DIM), bf16),
            pltpu.VMEM((heads, ROW + 1, 4, rows, HEAD_DIM), bf16),
            pltpu.VMEM((heads, PEERS, rows, HEAD_DIM), bf16),
            pltpu.VMEM((heads, PEERS, rows, HEAD_DIM), bf16),
            pltpu.VMEM((heads, 2, rows, HEAD_DIM), bf16),
            pltpu.VMEM((heads, HEAD_DIM, half), bf16),
            pltpu.VMEM((heads, HEAD_DIM, half), bf16),
            pltpu.VMEM((heads, 8, LANES), f32),
            pltpu.VMEM((heads, 8, LANES), f32),
            pltpu.VMEM((ROW + 1, 32, run_len), bf16),
            pltpu.VMEM((ROW + 1, run_len, LANES), bf16),
            pltpu.VMEM((2, ROW, run_len, LANES), bf16),
            pltpu.VMEM((2, ROW, 8, half), f32),
            pltpu.VMEM((2, ROW, 8, half), f32),
            pltpu.VMEM((2, ROW, HEAD_DIM, half), f32),
            dma((3, heads, ROW)), dma((3, heads)),
            dma((2, heads, ROW)), dma((2, heads)), dma((2, heads)),
            dma((2, heads)), dma((2, heads)),
            dma, dma((heads,)),
            dma, dma, dma, dma,
            dma((heads,)), dma((heads,)),
            dma((heads,)), dma((heads,)),
            dma((heads,)), dma((heads,)),
            pltpu.VMEM(token_order.shape, token_order.dtype),
            pltpu.VMEM(tile_mask.shape, tile_mask.dtype),
            dma((2,)),
        ],
        compiler_params=pltpu.CompilerParams(
            collective_id=0, has_side_effects=True, vmem_limit_bytes=56 * 1024 * 1024
        ),
        cost_estimate=pl.CostEstimate(
            flops=flops, bytes_accessed=8 * rows * width, transcendentals=flops // (4 * HEAD_DIM)
        ),
    )(queries, key_input, value_input, token_order, tile_mask)


def solution(mesh):
    in_specs = (
        P(("blk", "head"), None),
        P(("blk", "head"), None),
        P(("blk", "head"), None),
        P("blk"),
        P("blk", None),
    )
    out_specs = P(("blk", "head"), None)
    return jax.shard_map(local, mesh=mesh, in_specs=in_specs, out_specs=out_specs, check_vma=False)
```

```python
import functools
import math

import jax
import jax.numpy as jnp
from jax import lax
from jax.experimental import pallas as pl
from jax.experimental.pallas import tpu as pltpu
from jax.sharding import PartitionSpec as P

HEAD_DIM = 128
ROW = 4
PEERS = 2 * ROW
LANES = 128
HIDE = -(2.0**100)
MESH = pl.DeviceIdType.MESH


def kernel(
    heads, runs,
    q_in, k_in, v_in, order_in, mask_in,
    out,
    kbuf, vbuf, qbuf, obuf, q_far, o_far, o_back, log_far, log_back, info, km, qm, top_s, sum_s, acc_s,
    x_recv, x_send, z_recv, z_send, d_send, h_recv, h_send, o_recv, o_send, i_recv, i_send, ih_recv, ih_send,
    q_recv, q_send, p_recv, p_send, l_recv, l_send, order_ref, mask_ref, tile_sem,
):
    rows = q_in.shape[0]
    run_len = 4 * rows
    half = 2 * rows
    factor = math.log2(math.e) / math.sqrt(HEAD_DIM)
    last = ROW - 1

    blk = lax.axis_index("blk")
    head = lax.axis_index("head")
    x = lax.rem(blk, ROW)
    first = blk - x
    zl = lax.div(head, 2)
    core = lax.rem(head, 2)
    me = 2 * x + core
    across = 2 * (1 - zl)
    partner = (blk, across + core)
    mate = (lax.rem(blk + runs + (2 * zl - 1) * ROW, runs), across + core)
    own_edge = last * zl
    far_edge = last * (1 - zl)

    def device(peer):
        return (first + lax.div(peer, 2), 2 * zl + lax.rem(peer, 2))

    def peer_at(step):
        return lax.rem(me + step, PEERS)

    barrier = pltpu.get_barrier_semaphore()
    greet = [device(peer_at(step)) for step in range(1, PEERS)]
    greet += [partner, (blk, across + 1 - core), mate]
    for to in greet:
        pl.semaphore_signal(barrier, inc=1, device_id=to, device_id_type=MESH)

    order_copy = pltpu.make_async_copy(order_in, order_ref, tile_sem.at[0])
    mask_copy = pltpu.make_async_copy(mask_in, mask_ref, tile_sem.at[1])
    order_copy.start()
    mask_copy.start()
    order_copy.wait()
    mask_copy.wait()

    order = (order_ref[...].reshape(1, run_len) - blk * run_len).astype(jnp.float32)
    order = jnp.transpose(jnp.broadcast_to(order, (LANES, run_len)))[half:]
    lane = lax.broadcasted_iota(jnp.int32, (half, LANES), 1).astype(jnp.float32)
    second = jnp.concatenate(
        [
            jnp.sum(jnp.where(order == lane + LANES * g, 1.0, 0.0), axis=0, keepdims=True)
            for g in range(run_len // LANES)
        ],
        axis=1,
    )
    seen = mask_ref[...].astype(jnp.float32)
    mask_lane = lax.broadcasted_iota(jnp.int32, seen.shape, 1)

    def bias(offset):
        column = jnp.sum(jnp.where(mask_lane == 2 * blk + offset, seen, 0.0), axis=1, keepdims=True)
        return HIDE * (1.0 - (column[0:1] + second * (column[1:2] - column[0:1])))

    which = lax.broadcasted_iota(jnp.int32, (16, run_len), 0)
    log_row = lax.broadcasted_iota(jnp.int32, (8, LANES), 0)

    def stack(parts):
        total = jnp.zeros((16, run_len), jnp.float32)
        for index, part in enumerate(parts):
            total = jnp.where(which == index, part, total)
        return total.astype(jnp.bfloat16)

    mine = info.at[x]
    mine[0:16] = stack((1.0 - second, second, 1.0 - second, second))
    mine[16:32] = stack((bias(-2), bias(-1), bias(2), bias(3)))
    pl.semaphore_wait(barrier, len(greet))

    def columns(peer, j):
        return pl.ds(pl.multiple_of((heads * peer + j) * HEAD_DIM, HEAD_DIM), HEAD_DIM)

    def send(src, dst, send_sem, recv_sem, to):
        pltpu.make_async_remote_copy(
            src_ref=src, dst_ref=dst, send_sem=send_sem, recv_sem=recv_sem, device_id=to, device_id_type=MESH
        ).start()

    def wait(like, sem):
        pltpu.make_async_copy(like, like, sem).wait()

    sources = ((0, k_in, kbuf), (1, v_in, vbuf), (2, q_in, qbuf))

    def direct_start(j):
        for kind, source, buf in sources[:2]:
            for c in range(2):
                send(
                    source.at[:, columns(2 * x + c, j)], buf.at[j, x, head],
                    d_send.at[kind, j], z_recv.at[kind, j, x], (blk, across + c),
                )

    def x_start(j):
        for kind, source, buf in sources:
            place = qbuf.at[j, me] if kind == 2 else buf.at[j, x, head]
            pltpu.make_async_copy(source.at[:, columns(me, j)], place, x_recv.at[kind, j, x]).start()
            for step in range(1, PEERS):
                peer = peer_at(step)
                send(
                    source.at[:, columns(peer, j)], place,
                    x_send.at[kind, j], x_recv.at[kind, j, x], device(peer),
                )

    def unit(buf, j, run, side):
        return buf.at[j, run, pl.ds(2 * side, 2)]

    def halo_start(kind, buf, j, side):
        send(unit(buf, j, own_edge, side), unit(buf, j, ROW, side), h_send.at[kind, j], h_recv.at[kind, j], mate)

    def z_start(j, run):
        for kind, _, buf in sources[:2]:
            @pl.when(run != own_edge)
            def _():
                wait(unit(buf, j, run, zl), x_recv.at[kind, j, run])

            @pl.when((run != x) | (j == heads - 1))
            def _():
                send(
                    unit(buf, j, run, zl), unit(buf, j, run, zl),
                    z_send.at[kind, j], z_recv.at[kind, j, run], partner,
                )

    def queries_of(j, run):
        return qbuf.at[j, pl.ds(2 * run, 2)]

    def q_start(j):
        for run in range(ROW):
            wait(queries_of(j, run), x_recv.at[2, j, run])
        send(queries_of(j, far_edge), q_far.at[j], q_send.at[j], q_recv.at[j], partner)

    direct_start(0)
    x_start(0)
    for j in range(1, heads - 1):
        direct_start(j)

    for step in range(1, ROW):
        send(mine, mine, i_send, i_recv, (first + lax.rem(x + step, ROW), head))

    def spread(values):
        tall = jnp.concatenate([values, jnp.zeros((LANES - 16, run_len), jnp.float32)], axis=0)
        return jnp.transpose(tall).astype(jnp.bfloat16)

    def key_marks(slot):
        km[slot] = spread(info[slot, 0:16].astype(jnp.float32))

    def add_keys(state, q, marks, j, slot):
        top, total, acc = state
        k = kbuf[j, slot].reshape(run_len, HEAD_DIM)
        v = vbuf[j, slot].reshape(run_len, HEAD_DIM)
        if marks is not None:
            q = jnp.concatenate([q, marks], axis=1)
            k = jnp.concatenate([k, km[slot]], axis=1)
        scores = lax.dot_general(k, q, (((1,), (1,)), ((), ())), preferred_element_type=jnp.float32) * factor
        high = jnp.max(scores, axis=0, keepdims=True)
        new = high if top is None else jnp.maximum(top, high)
        weights = jnp.exp2(scores - new)
        part = jnp.sum(weights, axis=0, keepdims=True)
        mixed = lax.dot_general(
            v, weights.astype(jnp.bfloat16), (((0,), (0,)), ((), ())), preferred_element_type=jnp.float32
        )
        if top is None:
            return new, part, mixed
        fade = jnp.exp2(top - new)
        return new, total * fade + part, acc * fade + mixed

    def load(j, run):
        at = lax.rem(j, 2)
        return top_s[at, run][0:1], sum_s[at, run][0:1], acc_s[at, run]

    def store(state, j, run):
        at = lax.rem(j, 2)
        top, total, acc = state
        top_s[at, run] = jnp.broadcast_to(top, (8, half))
        sum_s[at, run] = jnp.broadcast_to(total, (8, half))
        acc_s[at, run] = acc

    def marks_of(side, run, of):
        return qm[side, run, pl.ds(pl.multiple_of(of * half, half), half)]

    def my_queries(j, run):
        return queries_of(j, run)[...].reshape(half, HEAD_DIM)

    def steps(j, slot, pairs):
        states = []
        for run, side in pairs:
            marks = None if side is None else marks_of(side, run, zl)
            states.append(add_keys(load(j, run), my_queries(j, run), marks, j, slot))
        for (run, _), state in zip(pairs, states):
            store(state, j, run)

    def finish(acc, total, j, run):
        rows_first = jnp.transpose(acc / total).astype(jnp.bfloat16)
        obuf[j, pl.ds(2 * run, 2)] = rows_first.reshape(2, rows, HEAD_DIM)
        for c in range(2):
            peer = 2 * run + c

            @pl.when(peer != me)
            def _():
                send(obuf.at[j, peer], out.at[:, columns(me, j)], o_send.at[j], o_recv, device(peer))

            @pl.when(peer == me)
            def _():
                pltpu.make_async_copy(obuf.at[j, peer], out.at[:, columns(me, j)], o_recv).start()

    def finish_run(j, run):
        _, total, acc = load(j, run)
        finish(acc, total, j, run)

    def outer(j):
        @pl.when(j == 0)
        def _():
            wait(info.at[ROW], ih_recv)
            key_marks(ROW)

        for kind, _, buf in sources[:2]:
            wait(buf.at[j, ROW], h_recv.at[kind, j])
        wait(q_far.at[j], q_recv.at[j])
        far = q_far[j].reshape(half, HEAD_DIM)
        top, total, acc = add_keys((None, None, None), far, marks_of(zl, own_edge, 1 - zl), j, ROW)
        state = add_keys(load(j, own_edge), my_queries(j, own_edge), marks_of(zl, own_edge, zl), j, ROW)
        o_far[j] = (acc / total).astype(jnp.bfloat16)
        logs = top + jnp.log2(total)
        packed = jnp.zeros((8, LANES), jnp.float32)
        for g in range(half // LANES):
            packed = jnp.where(log_row == g, logs[:, g * LANES : (g + 1) * LANES], packed)
        log_far[j] = packed
        send(o_far.at[j], o_back.at[j], p_send.at[j], p_recv.at[j], partner)
        send(log_far.at[j], log_back.at[j], l_send.at[j], l_recv.at[j], partner)
        finish(state[2], state[1], j, own_edge)

    def merge(j):
        wait(o_back.at[j], p_recv.at[j])
        wait(log_back.at[j], l_recv.at[j])
        top, total, acc = load(j, far_edge)
        logs = log_back[j]
        log = jnp.concatenate([logs[g : g + 1] for g in range(half // LANES)], axis=1)
        high = jnp.maximum(top, log)
        fade, other = jnp.exp2(top - high), jnp.exp2(log - high)
        finish(acc * fade + o_back[j].astype(jnp.float32) * other, total * fade + other, j, far_edge)

    def mirrored(index, flip):
        return index + flip * (last - 2 * index)

    def send_ahead(j, index):
        @pl.when(index == 0)
        def _():
            for kind, _, buf in sources[:2]:
                wait(unit(buf, j, own_edge, zl), x_recv.at[kind, j, own_edge])
                halo_start(kind, buf, j, zl)

        z_start(j, mirrored(index, 1 - zl))

        @pl.when(index == 1)
        def _():
            q_start(j)

            @pl.when(j + 1 < heads)
            def _():
                x_start(j + 1)

    def ahead_first(index, carry):
        send_ahead(0, index)
        return carry

    lax.fori_loop(0, ROW, ahead_first, 0)

    def drain_early(j, direct):
        for kind, _, buf in sources:
            wait(qbuf.at[j, pl.ds(0, PEERS - 1)], x_send.at[kind, j])
            if kind < 2:
                if direct:
                    wait(qbuf.at[j, pl.ds(0, 2)], d_send.at[kind, j])
                wait(buf.at[j, pl.ds(0, ROW - direct), pl.ds(0, 2)], z_send.at[kind, j])
                wait(buf.at[j, ROW], h_send.at[kind, j])
        wait(q_far.at[j], q_send.at[j])

    def drain_late(j):
        wait(qbuf.at[j, pl.ds(0, PEERS - 1)], o_send.at[j])
        wait(o_far.at[j], p_send.at[j])
        wait(log_far.at[j], l_send.at[j])

    def one_unit(t, carry):
        j = lax.div(t, ROW)
        index = lax.rem(t, ROW)
        run = mirrored(index, zl)

        @pl.when(j + 1 < heads)
        def _():
            send_ahead(j + 1, index)

        @pl.when(t == 0)
        def _():
            wait(info.at[pl.ds(0, ROW - 1)], i_recv)
            send(info.at[own_edge], info.at[ROW], ih_send, ih_recv, mate)
            for r in range(ROW):
                key_marks(r)
                marks = info[r, 16:32].astype(jnp.float32)
                qm[0, r] = spread(jnp.where(which < 2, marks, 0.0))
                qm[1, r] = spread(jnp.where(which >= 2, marks, 0.0))

        @pl.when(index == 0)
        def _():
            at = lax.rem(j, 2)
            top_s[at] = jnp.full((ROW, 8, half), 4.0 * HIDE, jnp.float32)
            sum_s[at] = jnp.zeros((ROW, 8, half), jnp.float32)
            acc_s[at] = jnp.zeros((ROW, HEAD_DIM, half), jnp.float32)

        @pl.when((index == 1) & (j > 0))
        def _():
            drain_early(j - 1, 1)

        @pl.when((index == 1) & (j > 1))
        def _():
            drain_late(j - 2)

        @pl.when((index == 2) & (j > 0))
        def _():
            merge(j - 1)

        @pl.when(index == 2)
        def _():
            outer(j)

        for kind, _, buf in sources[:2]:
            wait(unit(buf, j, run, 1 - zl), z_recv.at[kind, j, run])

        @pl.when(index == 0)
        def _():
            for kind, _, buf in sources[:2]:
                halo_start(kind, buf, j, 1 - zl)

        ahead, behind = (run + 1 - 2 * zl, zl), (run - 1 + 2 * zl, 1 - zl)

        @pl.when(index == 0)
        def _():
            steps(j, run, [ahead, (run, None)])

        @pl.when((index > 0) & (index < last))
        def _():
            steps(j, run, [behind, ahead, (run, None)])

        @pl.when(index == last)
        def _():
            steps(j, run, [behind, (run, None)])

        @pl.when(index >= 2)
        def _():
            finish_run(j, mirrored(index - 1, zl))

        return carry

    lax.fori_loop(0, heads * ROW, one_unit, 0)
    merge(heads - 1)
    drain_early(heads - 1, 0)
    if heads > 1:
        drain_late(heads - 2)
    wait(info.at[pl.ds(0, ROW - 1)], i_send)
    wait(info.at[0], ih_send)
    drain_late(heads - 1)
    wait(out, o_recv)


def local(queries, key_input, value_input, token_order, tile_mask):
    rows, width = queries.shape
    heads = width // HEAD_DIM // PEERS
    runs = lax.axis_size("blk")
    run_len = 4 * rows
    half = 2 * rows
    bf16, f32 = jnp.bfloat16, jnp.float32
    dma = pltpu.SemaphoreType.DMA
    hbm = pl.BlockSpec(memory_space=pl.ANY)
    vmem = pl.BlockSpec(memory_space=pltpu.VMEM)
    flops = 4 * heads * ROW * half * 3 * run_len * HEAD_DIM
    return pl.pallas_call(
        functools.partial(kernel, heads, runs),
        out_shape=pltpu.VMEM(queries.shape, queries.dtype),
        in_specs=[hbm] * 5,
        out_specs=vmem,
        scratch_shapes=[
            pltpu.VMEM((heads, ROW + 1, 4, rows, HEAD_DIM), bf16),
            pltpu.VMEM((heads, ROW + 1, 4, rows, HEAD_DIM), bf16),
            pltpu.VMEM((heads, PEERS, rows, HEAD_DIM), bf16),
            pltpu.VMEM((heads, PEERS, rows, HEAD_DIM), bf16),
            pltpu.VMEM((heads, 2, rows, HEAD_DIM), bf16),
            pltpu.VMEM((heads, HEAD_DIM, half), bf16),
            pltpu.VMEM((heads, HEAD_DIM, half), bf16),
            pltpu.VMEM((heads, 8, LANES), f32),
            pltpu.VMEM((heads, 8, LANES), f32),
            pltpu.VMEM((ROW + 1, 32, run_len), bf16),
            pltpu.VMEM((ROW + 1, run_len, LANES), bf16),
            pltpu.VMEM((2, ROW, run_len, LANES), bf16),
            pltpu.VMEM((2, ROW, 8, half), f32),
            pltpu.VMEM((2, ROW, 8, half), f32),
            pltpu.VMEM((2, ROW, HEAD_DIM, half), f32),
            dma((3, heads, ROW)), dma((3, heads)),
            dma((2, heads, ROW)), dma((2, heads)), dma((2, heads)),
            dma((2, heads)), dma((2, heads)),
            dma, dma((heads,)),
            dma, dma, dma, dma,
            dma((heads,)), dma((heads,)),
            dma((heads,)), dma((heads,)),
            dma((heads,)), dma((heads,)),
            pltpu.VMEM(token_order.shape, token_order.dtype),
            pltpu.VMEM(tile_mask.shape, tile_mask.dtype),
            dma((2,)),
        ],
        compiler_params=pltpu.CompilerParams(
            collective_id=0, has_side_effects=True, vmem_limit_bytes=56 * 1024 * 1024
        ),
        cost_estimate=pl.CostEstimate(
            flops=flops, bytes_accessed=8 * rows * width, transcendentals=flops // (4 * HEAD_DIM)
        ),
    )(queries, key_input, value_input, token_order, tile_mask)


def solution(mesh):
    in_specs = (
        P(("blk", "head"), None),
        P(("blk", "head"), None),
        P(("blk", "head"), None),
        P("blk"),
        P("blk", None),
    )
    out_specs = P(("blk", "head"), None)
    return jax.shard_map(local, mesh=mesh, in_specs=in_specs, out_specs=out_specs, check_vma=False)
```

```python
import functools
import math

import jax
import jax.numpy as jnp
from jax import lax
from jax.experimental import pallas as pl
from jax.experimental.pallas import tpu as pltpu
from jax.sharding import PartitionSpec as P

HEAD_DIM = 128
ROW = 4
PEERS = 2 * ROW
LANES = 128
HIDE = -(2.0**100)
MESH = pl.DeviceIdType.MESH


def kernel(
    heads, runs,
    q_in, k_in, v_in, order_in, mask_in,
    out,
    kbuf, vbuf, qbuf, obuf, q_far, o_far, o_back, log_far, log_back, info, km, qm, top_s, sum_s, acc_s,
    x_recv, x_send, z_recv, z_send, d_send, h_recv, h_send, o_recv, o_send, i_recv, i_send, ih_recv, ih_send,
    q_recv, q_send, p_recv, p_send, l_recv, l_send, order_ref, mask_ref, tile_sem,
):
    rows = q_in.shape[0]
    run_len = 4 * rows
    half = 2 * rows
    factor = math.log2(math.e) / math.sqrt(HEAD_DIM)
    last = ROW - 1

    blk = lax.axis_index("blk")
    head = lax.axis_index("head")
    x = lax.rem(blk, ROW)
    first = blk - x
    zl = lax.div(head, 2)
    core = lax.rem(head, 2)
    me = 2 * x + core
    across = 2 * (1 - zl)
    partner = (blk, across + core)
    mate = (lax.rem(blk + runs + (2 * zl - 1) * ROW, runs), across + core)
    own_edge = last * zl
    far_edge = last * (1 - zl)

    def device(peer):
        return (first + lax.div(peer, 2), 2 * zl + lax.rem(peer, 2))

    def peer_at(step):
        return lax.rem(me + step, PEERS)

    barrier = pltpu.get_barrier_semaphore()
    greet = [device(peer_at(step)) for step in range(1, PEERS)]
    greet += [partner, (blk, across + 1 - core), mate]
    for to in greet:
        pl.semaphore_signal(barrier, inc=1, device_id=to, device_id_type=MESH)

    order_copy = pltpu.make_async_copy(order_in, order_ref, tile_sem.at[0])
    mask_copy = pltpu.make_async_copy(mask_in, mask_ref, tile_sem.at[1])
    order_copy.start()
    mask_copy.start()
    pl.semaphore_wait(barrier, len(greet))

    def columns(peer, j):
        return pl.ds(pl.multiple_of((heads * peer + j) * HEAD_DIM, HEAD_DIM), HEAD_DIM)

    def send(src, dst, send_sem, recv_sem, to):
        pltpu.make_async_remote_copy(
            src_ref=src, dst_ref=dst, send_sem=send_sem, recv_sem=recv_sem, device_id=to, device_id_type=MESH
        ).start()

    def wait(like, sem):
        pltpu.make_async_copy(like, like, sem).wait()

    sources = ((0, k_in, kbuf), (1, v_in, vbuf), (2, q_in, qbuf))

    def direct_start(j):
        for kind, source, buf in sources[:2]:
            for c in range(2):
                send(
                    source.at[:, columns(2 * x + c, j)], buf.at[j, x, head],
                    d_send.at[kind, j], z_recv.at[kind, j, x], (blk, across + c),
                )

    def x_start(j):
        for kind, source, buf in sources:
            place = qbuf.at[j, me] if kind == 2 else buf.at[j, x, head]
            pltpu.make_async_copy(source.at[:, columns(me, j)], place, x_recv.at[kind, j, x]).start()
            for step in range(1, PEERS):
                peer = peer_at(step)
                send(
                    source.at[:, columns(peer, j)], place,
                    x_send.at[kind, j], x_recv.at[kind, j, x], device(peer),
                )

    def unit(buf, j, run, side):
        return buf.at[j, run, pl.ds(2 * side, 2)]

    def halo_start(kind, buf, j, side):
        send(unit(buf, j, own_edge, side), unit(buf, j, ROW, side), h_send.at[kind, j], h_recv.at[kind, j], mate)

    def z_start(j, run):
        for kind, _, buf in sources[:2]:
            @pl.when(run != own_edge)
            def _():
                wait(unit(buf, j, run, zl), x_recv.at[kind, j, run])

            @pl.when((run != x) | (j == heads - 1))
            def _():
                send(
                    unit(buf, j, run, zl), unit(buf, j, run, zl),
                    z_send.at[kind, j], z_recv.at[kind, j, run], partner,
                )

    def queries_of(j, run):
        return qbuf.at[j, pl.ds(2 * run, 2)]

    def q_start(j):
        for run in range(ROW):
            wait(queries_of(j, run), x_recv.at[2, j, run])
        send(queries_of(j, far_edge), q_far.at[j], q_send.at[j], q_recv.at[j], partner)

    direct_start(0)
    x_start(0)
    for j in range(1, heads - 1):
        direct_start(j)

    order_copy.wait()
    mask_copy.wait()

    order = (order_ref[...].reshape(1, run_len) - blk * run_len).astype(jnp.float32)
    order = jnp.transpose(jnp.broadcast_to(order, (LANES, run_len)))[half:]
    lane = lax.broadcasted_iota(jnp.int32, (half, LANES), 1).astype(jnp.float32)
    second = jnp.concatenate(
        [
            jnp.sum(jnp.where(order == lane + LANES * g, 1.0, 0.0), axis=0, keepdims=True)
            for g in range(run_len // LANES)
        ],
        axis=1,
    )
    seen = mask_ref[...].astype(jnp.float32)
    mask_lane = lax.broadcasted_iota(jnp.int32, seen.shape, 1)

    def bias(offset):
        column = jnp.sum(jnp.where(mask_lane == 2 * blk + offset, seen, 0.0), axis=1, keepdims=True)
        return HIDE * (1.0 - (column[0:1] + second * (column[1:2] - column[0:1])))

    which = lax.broadcasted_iota(jnp.int32, (16, run_len), 0)
    log_row = lax.broadcasted_iota(jnp.int32, (8, LANES), 0)

    def stack(parts):
        total = jnp.zeros((16, run_len), jnp.float32)
        for index, part in enumerate(parts):
            total = jnp.where(which == index, part, total)
        return total.astype(jnp.bfloat16)

    mine = info.at[x]
    mine[0:16] = stack((1.0 - second, second, 1.0 - second, second))
    mine[16:32] = stack((bias(-2), bias(-1), bias(2), bias(3)))

    for step in range(1, ROW):
        send(mine, mine, i_send, i_recv, (first + lax.rem(x + step, ROW), head))

    def spread(values):
        tall = jnp.concatenate([values, jnp.zeros((LANES - 16, run_len), jnp.float32)], axis=0)
        return jnp.transpose(tall).astype(jnp.bfloat16)

    def key_marks(slot):
        km[slot] = spread(info[slot, 0:16].astype(jnp.float32))

    def add_keys(state, q, marks, j, slot):
        top, total, acc = state
        k = kbuf[j, slot].reshape(run_len, HEAD_DIM)
        v = vbuf[j, slot].reshape(run_len, HEAD_DIM)
        if marks is not None:
            q = jnp.concatenate([q, marks], axis=1)
            k = jnp.concatenate([k, km[slot]], axis=1)
        scores = lax.dot_general(k, q, (((1,), (1,)), ((), ())), preferred_element_type=jnp.float32) * factor
        high = jnp.max(scores, axis=0, keepdims=True)
        new = high if top is None else jnp.maximum(top, high)
        weights = jnp.exp2(scores - new)
        part = jnp.sum(weights, axis=0, keepdims=True)
        mixed = lax.dot_general(
            v, weights.astype(jnp.bfloat16), (((0,), (0,)), ((), ())), preferred_element_type=jnp.float32
        )
        if top is None:
            return new, part, mixed
        fade = jnp.exp2(top - new)
        return new, total * fade + part, acc * fade + mixed

    def load(j, run):
        at = lax.rem(j, 2)
        return top_s[at, run][0:1], sum_s[at, run][0:1], acc_s[at, run]

    def store(state, j, run):
        at = lax.rem(j, 2)
        top, total, acc = state
        top_s[at, run] = jnp.broadcast_to(top, (8, half))
        sum_s[at, run] = jnp.broadcast_to(total, (8, half))
        acc_s[at, run] = acc

    def marks_of(side, run, of):
        return qm[side, run, pl.ds(pl.multiple_of(of * half, half), half)]

    def my_queries(j, run):
        return queries_of(j, run)[...].reshape(half, HEAD_DIM)

    def steps(j, slot, pairs):
        states = []
        for run, side in pairs:
            marks = None if side is None else marks_of(side, run, zl)
            states.append(add_keys(load(j, run), my_queries(j, run), marks, j, slot))
        for (run, _), state in zip(pairs, states):
            store(state, j, run)

    def finish(acc, total, j, run):
        rows_first = jnp.transpose(acc / total).astype(jnp.bfloat16)
        obuf[j, pl.ds(2 * run, 2)] = rows_first.reshape(2, rows, HEAD_DIM)
        for c in range(2):
            peer = 2 * run + c

            @pl.when(peer != me)
            def _():
                send(obuf.at[j, peer], out.at[:, columns(me, j)], o_send.at[j], o_recv, device(peer))

            @pl.when(peer == me)
            def _():
                pltpu.make_async_copy(obuf.at[j, peer], out.at[:, columns(me, j)], o_recv).start()

    def finish_run(j, run):
        _, total, acc = load(j, run)
        finish(acc, total, j, run)

    def outer(j):
        @pl.when(j == 0)
        def _():
            wait(info.at[ROW], ih_recv)
            key_marks(ROW)

        for kind, _, buf in sources[:2]:
            wait(buf.at[j, ROW], h_recv.at[kind, j])
        wait(q_far.at[j], q_recv.at[j])
        far = q_far[j].reshape(half, HEAD_DIM)
        top, total, acc = add_keys((None, None, None), far, marks_of(zl, own_edge, 1 - zl), j, ROW)
        o_far[j] = (acc / total).astype(jnp.bfloat16)
        logs = top + jnp.log2(total)
        packed = jnp.zeros((8, LANES), jnp.float32)
        for g in range(half // LANES):
            packed = jnp.where(log_row == g, logs[:, g * LANES : (g + 1) * LANES], packed)
        log_far[j] = packed
        send(o_far.at[j], o_back.at[j], p_send.at[j], p_recv.at[j], partner)
        send(log_far.at[j], log_back.at[j], l_send.at[j], l_recv.at[j], partner)
        state = add_keys(load(j, own_edge), my_queries(j, own_edge), marks_of(zl, own_edge, zl), j, ROW)
        finish(state[2], state[1], j, own_edge)

    def merge(j):
        wait(o_back.at[j], p_recv.at[j])
        wait(log_back.at[j], l_recv.at[j])
        top, total, acc = load(j, far_edge)
        logs = log_back[j]
        log = jnp.concatenate([logs[g : g + 1] for g in range(half // LANES)], axis=1)
        high = jnp.maximum(top, log)
        fade, other = jnp.exp2(top - high), jnp.exp2(log - high)
        finish(acc * fade + o_back[j].astype(jnp.float32) * other, total * fade + other, j, far_edge)

    def mirrored(index, flip):
        return index + flip * (last - 2 * index)

    def send_ahead(j, index):
        @pl.when(index == 0)
        def _():
            for kind, _, buf in sources[:2]:
                wait(unit(buf, j, own_edge, zl), x_recv.at[kind, j, own_edge])
                halo_start(kind, buf, j, zl)

        z_start(j, mirrored(index, 1 - zl))

        @pl.when(index == 1)
        def _():
            q_start(j)

            @pl.when(j + 1 < heads)
            def _():
                x_start(j + 1)

    def ahead_first(index, carry):
        send_ahead(0, index)
        return carry

    lax.fori_loop(0, ROW, ahead_first, 0)

    def drain_early(j, direct):
        for kind, _, buf in sources:
            wait(qbuf.at[j, pl.ds(0, PEERS - 1)], x_send.at[kind, j])
            if kind < 2:
                if direct:
                    wait(qbuf.at[j, pl.ds(0, 2)], d_send.at[kind, j])
                wait(buf.at[j, pl.ds(0, ROW - direct), pl.ds(0, 2)], z_send.at[kind, j])
                wait(buf.at[j, ROW], h_send.at[kind, j])
        wait(q_far.at[j], q_send.at[j])

    def drain_late(j):
        wait(qbuf.at[j, pl.ds(0, PEERS - 1)], o_send.at[j])
        wait(o_far.at[j], p_send.at[j])
        wait(log_far.at[j], l_send.at[j])

    def one_unit(t, carry):
        j = lax.div(t, ROW)
        index = lax.rem(t, ROW)
        run = mirrored(index, zl)

        @pl.when(j + 1 < heads)
        def _():
            send_ahead(j + 1, index)

        @pl.when(t == 0)
        def _():
            wait(info.at[pl.ds(0, ROW - 1)], i_recv)
            send(info.at[own_edge], info.at[ROW], ih_send, ih_recv, mate)
            for r in range(ROW):
                key_marks(r)
                marks = info[r, 16:32].astype(jnp.float32)
                qm[0, r] = spread(jnp.where(which < 2, marks, 0.0))
                qm[1, r] = spread(jnp.where(which >= 2, marks, 0.0))

        @pl.when(index == 0)
        def _():
            at = lax.rem(j, 2)
            top_s[at] = jnp.full((ROW, 8, half), 4.0 * HIDE, jnp.float32)
            sum_s[at] = jnp.zeros((ROW, 8, half), jnp.float32)
            acc_s[at] = jnp.zeros((ROW, HEAD_DIM, half), jnp.float32)

        @pl.when((index == 1) & (j > 0))
        def _():
            drain_early(j - 1, 1)

        @pl.when((index == 1) & (j > 1))
        def _():
            drain_late(j - 2)

        @pl.when((index == 2) & (j > 0))
        def _():
            merge(j - 1)

        @pl.when(index == 2)
        def _():
            outer(j)

        for kind, _, buf in sources[:2]:
            wait(unit(buf, j, run, 1 - zl), z_recv.at[kind, j, run])

        @pl.when(index == 0)
        def _():
            for kind, _, buf in sources[:2]:
                halo_start(kind, buf, j, 1 - zl)

        ahead, behind = (run + 1 - 2 * zl, zl), (run - 1 + 2 * zl, 1 - zl)

        @pl.when(index == 0)
        def _():
            steps(j, run, [ahead, (run, None)])

        @pl.when((index > 0) & (index < last))
        def _():
            steps(j, run, [behind, ahead, (run, None)])

        @pl.when(index == last)
        def _():
            steps(j, run, [behind, (run, None)])

        @pl.when(index >= 2)
        def _():
            finish_run(j, mirrored(index - 1, zl))

        return carry

    lax.fori_loop(0, heads * ROW, one_unit, 0)
    merge(heads - 1)
    drain_early(heads - 1, 0)
    if heads > 1:
        drain_late(heads - 2)
    wait(info.at[pl.ds(0, ROW - 1)], i_send)
    wait(info.at[0], ih_send)
    drain_late(heads - 1)
    wait(out, o_recv)


def local(queries, key_input, value_input, token_order, tile_mask):
    rows, width = queries.shape
    heads = width // HEAD_DIM // PEERS
    runs = lax.axis_size("blk")
    run_len = 4 * rows
    half = 2 * rows
    bf16, f32 = jnp.bfloat16, jnp.float32
    dma = pltpu.SemaphoreType.DMA
    hbm = pl.BlockSpec(memory_space=pl.ANY)
    vmem = pl.BlockSpec(memory_space=pltpu.VMEM)
    flops = 4 * heads * ROW * half * 3 * run_len * HEAD_DIM
    return pl.pallas_call(
        functools.partial(kernel, heads, runs),
        out_shape=pltpu.VMEM(queries.shape, queries.dtype),
        in_specs=[hbm] * 5,
        out_specs=vmem,
        scratch_shapes=[
            pltpu.VMEM((heads, ROW + 1, 4, rows, HEAD_DIM), bf16),
            pltpu.VMEM((heads, ROW + 1, 4, rows, HEAD_DIM), bf16),
            pltpu.VMEM((heads, PEERS, rows, HEAD_DIM), bf16),
            pltpu.VMEM((heads, PEERS, rows, HEAD_DIM), bf16),
            pltpu.VMEM((heads, 2, rows, HEAD_DIM), bf16),
            pltpu.VMEM((heads, HEAD_DIM, half), bf16),
            pltpu.VMEM((heads, HEAD_DIM, half), bf16),
            pltpu.VMEM((heads, 8, LANES), f32),
            pltpu.VMEM((heads, 8, LANES), f32),
            pltpu.VMEM((ROW + 1, 32, run_len), bf16),
            pltpu.VMEM((ROW + 1, run_len, LANES), bf16),
            pltpu.VMEM((2, ROW, run_len, LANES), bf16),
            pltpu.VMEM((2, ROW, 8, half), f32),
            pltpu.VMEM((2, ROW, 8, half), f32),
            pltpu.VMEM((2, ROW, HEAD_DIM, half), f32),
            dma((3, heads, ROW)), dma((3, heads)),
            dma((2, heads, ROW)), dma((2, heads)), dma((2, heads)),
            dma((2, heads)), dma((2, heads)),
            dma, dma((heads,)),
            dma, dma, dma, dma,
            dma((heads,)), dma((heads,)),
            dma((heads,)), dma((heads,)),
            dma((heads,)), dma((heads,)),
            pltpu.VMEM(token_order.shape, token_order.dtype),
            pltpu.VMEM(tile_mask.shape, tile_mask.dtype),
            dma((2,)),
        ],
        compiler_params=pltpu.CompilerParams(
            collective_id=0, has_side_effects=True, vmem_limit_bytes=56 * 1024 * 1024
        ),
        cost_estimate=pl.CostEstimate(
            flops=flops, bytes_accessed=8 * rows * width, transcendentals=flops // (4 * HEAD_DIM)
        ),
    )(queries, key_input, value_input, token_order, tile_mask)


def solution(mesh):
    in_specs = (
        P(("blk", "head"), None),
        P(("blk", "head"), None),
        P(("blk", "head"), None),
        P("blk"),
        P("blk", None),
    )
    out_specs = P(("blk", "head"), None)
    return jax.shard_map(local, mesh=mesh, in_specs=in_specs, out_specs=out_specs, check_vma=False)
```
